256 devices in a mesh: prow: 64 (over z, y, core), pcol: 4 (over x).
Axes of the slice: x: 4, y: 4, z: 8, core: 2. Of those that a mesh axis runs over, the one named last changes fastest.
Arguments:
- matrix: bfloat16 [32768, 20480], P('prow', 'pcol')
- pivots: int32 [2, 256], replicated, may hold values from 0 to 32767, as said below
Outputs:
- factored: bfloat16 [32768, 20480], P('prow', 'pcol')
The draws below stay inside these ranges and needn't reach their ends.
Inputs may be any that keep to these rules, and one draw needn't show every extreme that they name: `pivots`: each list holds 256 distinct row indices; no index appears in two lists. The rows k * 2 * 256 to (k + 1) * 2 * 256 - 1 hold at most 8 entries of one list, and some such k holds exactly 8 in every list. The pivot rows of each panel give its diagonal block a diagonal large enough, relative to its other entries, that the Newton-Schulz steps converge.
All inputs are finite; a program needn't handle non-finite values.
Results may differ from the reference program's by a relative error of at most 0.001.
Values may be sent and summed in bfloat16 or wider, within the bound.
No kernel may reach another device: no remote copies, remote signals or barrier semaphores. Data moves between devices by JAX's collectives and lax.ppermute only.
A program may use at most 64 MiB of HBM per device.

```python
import math
import jax
import jax.numpy as jnp
from jax import lax

NB = 256
LB = 2
NCOLS = 20480
PANELS = 2
NEWTON = 3
M = 32768
BC = 20
N_PCOL = 4


def pivot_lists(key):
    key = jax.random.fold_in(key, 500)
    rows_dev = LB * NB
    groups = M // rows_dev
    base = NB // groups
    cap = 2 * base
    keys = jax.random.split(jax.random.fold_in(key, 1), groups)
    orders = jax.vmap(lambda each: jax.random.permutation(each, rows_dev))(keys).astype(jnp.int32)
    offsets = jnp.zeros((groups,), jnp.int32)
    slots = jnp.arange(cap, dtype=jnp.int32)
    lists = []
    for panel in range(PANELS):
        first_key, second_key, third_key = jax.random.split(jax.random.fold_in(key, 10 + panel), 3)
        shuffle_groups = jax.random.permutation(first_key, groups)
        half = groups // 2
        shifts = jax.random.randint(second_key, (half,), 0, base + 1).astype(jnp.int32).at[0].set(base)
        counts = jnp.zeros((groups,), jnp.int32)
        counts = counts.at[shuffle_groups[:half]].set(base + shifts)
        counts = counts.at[shuffle_groups[half:]].set(base - shifts)
        picks = offsets[:, None] + slots[None, :]
        local_rows = jnp.take_along_axis(orders, picks, axis=1)
        valid = slots[None, :] < counts[:, None]
        global_rows = local_rows + (jnp.arange(groups, dtype=jnp.int32) * rows_dev)[:, None]
        flat_rows = global_rows.reshape(-1)
        score = jnp.where(valid.reshape(-1), 0, 1) * (groups * cap) + jnp.arange(groups * cap, dtype=jnp.int32)
        picked = flat_rows[jnp.argsort(score)[:NB]]
        lists.append(picked[jax.random.permutation(third_key, NB)])
        offsets = offsets + counts
    return jnp.stack(lists).astype(jnp.int32)


def draw_pivots(key, part):
    return pivot_lists(key)


def draw_matrix(key, part):
    lists = pivot_lists(key)
    key = jax.random.fold_in(key, 3)
    noise_key, sign_key, size_key = jax.random.split(key, 3)
    spread = 0.25
    noise = jax.random.truncated_normal(noise_key, -6.0, 6.0, (M, NCOLS), jnp.float32) * spread
    for panel in range(PANELS):
        low = 12.0 if panel == 0 else 60.0
        high = 24.0 if panel == 0 else 120.0
        signs = jnp.where(jax.random.bernoulli(jax.random.fold_in(sign_key, panel), 0.5, (NB,)), 1.0, -1.0)
        sizes = jnp.exp(jax.random.uniform(jax.random.fold_in(size_key, panel), (NB,), jnp.float32, math.log(low), math.log(high)))
        columns = panel * BC * NB + jnp.arange(NB, dtype=jnp.int32)
        noise = noise.at[lists[panel], columns].set(signs * sizes)
    return noise.astype(jnp.bfloat16)


def setup_inputs(seed: int = 0) -> dict:
    seeds = jax.random.split(jax.random.key(seed), 3)
    matrix = draw_matrix(jax.random.fold_in(seeds[2], 71), 0)
    pivots = draw_pivots(jax.random.fold_in(seeds[2], 71), 0)
    return {"matrix": matrix, "pivots": pivots}


def inverse(block):
    guess = jnp.diag(1.0 / jnp.diagonal(block))
    twice = 2.0 * jnp.eye(block.shape[0], dtype=jnp.float32)
    for step in range(NEWTON):
        inner = twice - jnp.dot(block, guess, precision=lax.Precision.HIGHEST)
        guess = jnp.dot(guess, inner, precision=lax.Precision.HIGHEST)
    return guess


def reference(matrix, pivots):
    rows_dev = LB * NB
    groups = M // rows_dev
    block_ids = jnp.arange(NCOLS, dtype=jnp.int32) // NB
    logical = (block_ids % BC) * N_PCOL + block_ids // BC
    used = jnp.zeros((M,), dtype=bool)
    current = matrix
    for panel in range(PANELS):
        lead = panel * BC * NB
        chosen = pivots[panel]
        used = used.at[chosen].set(True)
        upper = jnp.take(current, chosen, axis=0)
        inv = inverse(upper[:, lead:lead + NB].astype(jnp.float32))
        later = logical > panel
        active = jnp.logical_not(used).reshape(groups, rows_dev)

        def one(pair):
            rows, live = pair
            left = jnp.dot(rows[:, lead:lead + NB].astype(jnp.float32), inv, precision=lax.Precision.HIGHEST)
            left = jnp.where(live[:, None], left, 0.0).astype(jnp.bfloat16)
            product = jnp.dot(left, upper, preferred_element_type=jnp.float32)
            fresh = (rows.astype(jnp.float32) - product).astype(jnp.bfloat16)
            result = jnp.where(live[:, None] & later[None, :], fresh, rows)
            return result.at[:, lead:lead + NB].set(jnp.where(live[:, None], left, rows[:, lead:lead + NB]))

        current = lax.map(one, (current.reshape(groups, rows_dev, NCOLS), active)).reshape(M, NCOLS)
    return current
```

```python
import functools
import jax
import jax.numpy as jnp
from jax import lax
from jax.experimental import pallas as pl
from jax.experimental.pallas import tpu as pltpu
from jax.sharding import PartitionSpec as P

NB = 256
NEWTON = 3
ZN, YN = 8, 4
CAP = 8
SLOTS = 2 * CAP
CHIP = 2 * SLOTS
WZ = 2560
F32 = jnp.float32
BF16 = jnp.bfloat16
VMEM = pl.BlockSpec(memory_space=pltpu.VMEM)
SMEM = pl.BlockSpec(memory_space=pltpu.SMEM)
ANY = pl.BlockSpec(memory_space=pl.ANY)
HBM = pl.BlockSpec(memory_space=pltpu.HBM)
PARAMS = pltpu.CompilerParams(vmem_limit_bytes=16 * 2**20)


def moves(dz, dy):
    pairs = []
    for z in range(ZN):
        for y in range(YN):
            for core in range(2):
                sign = 1 - 2 * core
                there = ((z + sign * dz) % ZN) * YN + (y + sign * dy) % YN
                pairs.append(((z * YN + y) * 2 + core, there * 2 + core))
    return pairs


ALONG_Z = moves(1, 0)
ALONG_Y = moves(0, 1)
TWICE_Y = moves(0, 2)
PAIR = [(i, i ^ 1) for i in range(2 * ZN * YN)]


NEAR = [(0, 1), (1, 0)]
FAR = [(0, 3), (1, 2)]
SKIP = [(0, 2), (1, 3)]
ACROSS = [(2, 3), (3, 2)]


def over(array, pairs):
    return lax.ppermute(array, "pcol", pairs)


def send(array, pairs):
    return lax.ppermute(array, "prow", pairs)


def after(array, *others):
    return lax.optimization_barrier((array, *others))[0]


def both(*arrays):
    return lax.optimization_barrier(arrays)


def iota(shape, dim):
    return lax.broadcasted_iota(jnp.int32, shape, dim)


def to_column(row):
    n = row.shape[1]
    eye = iota((n, n), 0) == iota((n, n), 1)
    return jnp.sum(jnp.where(eye, row, 0.0), axis=1, keepdims=True)


def slot_column(piv_row, rows_dev):
    n = piv_row.shape[1]
    owner_row = lax.div(piv_row, jnp.int32(rows_dev)).astype(F32)
    owner_col = to_column(owner_row)
    before = iota((n, n), 1) < iota((n, n), 0)
    rank = jnp.sum(jnp.where(before & (owner_row == owner_col), 1.0, 0.0), axis=1, keepdims=True)
    return owner_col * CAP + rank


def chip_slots(me, order):
    n = ZN * YN * SLOTS
    pos = iota((1, n), 1)
    block = pos // SLOTS
    chip = me // 2
    z, y = chip // YN, chip % YN
    sign = 2 * (me % 2) - 1
    if order == "z first":
        zz = (z - block % ZN) & (ZN - 1)
        yy = (y + sign * (block // ZN)) & (YN - 1)
    else:
        yy = (y - block % YN) & (YN - 1)
        zz = (z + sign * (block // YN)) & (ZN - 1)
    return ((zz * YN + yy) * SLOTS + pos % SLOTS).astype(F32)


def is_pivot(piv_row, me, rows_dev):
    local = piv_row - me * rows_dev
    hit = iota((rows_dev, piv_row.shape[1]), 0) == local
    return jnp.max(jnp.where(hit, 1.0, 0.0), axis=1, keepdims=True) > 0.5


def list_rows(blocks, which):
    parts = []
    for block in blocks:
        rows, width = block.shape
        chips = rows // CHIP
        parts.append(block.reshape(chips, 2, SLOTS, width)[:, which].reshape(chips * SLOTS, width))
    return jnp.concatenate(parts, axis=0) if len(parts) > 1 else parts[0]


def dot(a, b):
    return jnp.dot(a, b, preferred_element_type=F32)


def dot_high(a, b):
    return jnp.dot(a, b, precision=lax.Precision.HIGHEST, preferred_element_type=F32)


def pieces(b):
    high = b.astype(BF16)
    rest = b - high.astype(F32)
    middle = rest.astype(BF16)
    return high, middle, (rest - middle.astype(F32)).astype(BF16)


def dot_exact(a, parts):
    high, middle, low = parts
    return dot(a, high) + (dot(a, middle) + dot(a, low))


def pick_kernel(chunk, ids, piv_ref, a_hbm, out_ref, a_ref, sems):
    me = ids[0]
    chunks, rows_dev, _ = a_ref.shape

    def fetch(k):
        return pltpu.make_async_copy(
            a_hbm.at[:, pl.ds(k * chunk, chunk)], a_ref.at[k], sems.at[k]
        )

    for k in range(chunks):
        fetch(k).start()
    hots = []
    for which in range(2):
        piv_row = piv_ref[which : which + 1, :]
        n = piv_row.shape[1]
        owner_row = lax.div(piv_row, jnp.int32(rows_dev)).astype(F32)
        owner_col = to_column(owner_row)
        before = iota((n, n), 0) < iota((n, n), 1)
        rank = jnp.sum(jnp.where(before & (owner_row == owner_col), 1.0, 0.0), axis=0, keepdims=True)
        slot = rank + ((me % 2) * CAP).astype(F32)
        mine = owner_row == me.astype(F32)
        place = mine & (iota((SLOTS, n), 0).astype(F32) == slot)
        local = to_column((piv_row - me * rows_dev).astype(F32))
        row = local == iota((n, rows_dev), 1).astype(F32)
        hot = dot(jnp.where(place, 1.0, 0.0).astype(BF16), jnp.where(row, 1.0, 0.0).astype(BF16))
        hots.append(hot)
    hot = jnp.concatenate(hots, axis=0).astype(BF16)
    for k in range(chunks):
        fetch(k).wait()
        out_ref[:, k * chunk : (k + 1) * chunk] = dot(hot, a_ref[k]).astype(BF16)


def pick(ids, pivots, matrix):
    rows_dev, width = matrix.shape
    chunk = 1024
    chunks = width // chunk
    return pl.pallas_call(
        functools.partial(pick_kernel, chunk),
        in_specs=[SMEM, VMEM, HBM],
        out_specs=VMEM,
        out_shape=jax.ShapeDtypeStruct((CHIP, width), BF16),
        scratch_shapes=[
            pltpu.VMEM((chunks, rows_dev, chunk), BF16),
            pltpu.SemaphoreType.DMA((chunks,)),
        ],
        compiler_params=PARAMS,
        cost_estimate=pl.CostEstimate(
            flops=2 * CHIP * rows_dev * width, bytes_accessed=4 * rows_dev * width, transcendentals=0
        ),
        name="pick",
    )(ids, pivots, pltpu.with_memory_space_constraint(matrix, pltpu.HBM))


def maps_kernel(rows_dev, ids, piv_ref, *out_refs):
    me = ids[0]
    for which in range(2):
        slots = slot_column(piv_ref[which : which + 1, :], rows_dev)
        rows = slice(which * NB, (which + 1) * NB)
        for order, out in zip(("z first", "y first"), out_refs):
            out[rows, :] = jnp.where(slots == chip_slots(me, order), 1.0, 0.0).astype(BF16)


def maps(ids, pivots, rows_dev):
    shape = jax.ShapeDtypeStruct((2 * NB, ZN * YN * SLOTS), BF16)
    return pl.pallas_call(
        functools.partial(maps_kernel, rows_dev),
        in_specs=[SMEM, VMEM],
        out_specs=[VMEM] * 2,
        out_shape=[shape] * 2,
        cost_estimate=pl.CostEstimate(flops=2**30, bytes_accessed=2**22, transcendentals=0),
        name="maps",
    )(ids, pivots)


def inverse(block):
    n = block.shape[0]
    wide = block.astype(F32)
    eye = iota((n, n), 0) == iota((n, n), 1)
    diagonal_row = jnp.sum(jnp.where(eye, wide, 0.0), axis=0, keepdims=True)
    diagonal_col = jnp.sum(jnp.where(eye, wide, 0.0), axis=1, keepdims=True)
    twice = jnp.where(eye, 2.0, 0.0)
    guess = (1.0 / diagonal_col) * (twice - wide * (1.0 / diagonal_row))
    for step in range(NEWTON - 1):
        inner = twice - dot_exact(block, pieces(guess))
        guess = dot_high(guess, inner)
    return guess


def factor_kernel(ids, piv_ref, s0_ref, s1_ref, pan0_ref, pan1_ref, l0_ref, l1_ref, lp_ref, fin_ref):
    me, col = ids[0], ids[1]
    rows_dev = pan0_ref.shape[0]
    upper01 = s1_ref[:NB, :]
    inv0 = pieces(inverse(s0_ref[:NB, :]))
    lower = dot_exact(s0_ref[NB:, :], inv0).astype(BF16)
    lp_ref[...] = lower
    block1 = (s1_ref[NB:, :].astype(F32) - dot(lower, upper01)).astype(BF16)
    inv1 = pieces(inverse(block1))
    live0 = jnp.logical_not(is_pivot(piv_ref[0:1, :], me, rows_dev))
    live1 = live0 & jnp.logical_not(is_pivot(piv_ref[1:2, :], me, rows_dev))
    pan0 = pan0_ref[...]
    left0 = jnp.where(live0, dot_exact(pan0, inv0), 0.0).astype(BF16)
    l0_ref[...] = left0
    pan1 = (pan1_ref[...].astype(F32) - dot(left0, upper01)).astype(BF16)
    left1 = jnp.where(live1, dot_exact(pan1, inv1), 0.0).astype(BF16)
    l1_ref[...] = left1
    fin0 = jnp.where(live0, left0.astype(F32), pan0.astype(F32))
    fin1 = jnp.where(live1, left1.astype(F32), pan1.astype(F32))
    fin_ref[...] = jnp.where(col == 0, fin0, fin1).astype(BF16)


def factor(ids, pivots, uppers, pan0, pan1):
    rows_dev = pan0.shape[0]
    left = jax.ShapeDtypeStruct((rows_dev, NB), BF16)
    return pl.pallas_call(
        factor_kernel,
        in_specs=[SMEM] + [VMEM] * 5,
        out_specs=[VMEM] * 4,
        out_shape=[left, left, jax.ShapeDtypeStruct((NB, NB), BF16), left],
        compiler_params=PARAMS,
        cost_estimate=pl.CostEstimate(
            flops=2 * 3 * 64 * NB**3, bytes_accessed=4 * 2**20, transcendentals=0
        ),
        name="factor",
    )(ids, pivots, *uppers, pan0, pan1)


def step_of(width):
    if width < 512:
        return width
    return 640 if width % 1280 == 0 else 512


def select_kernel(spans, hot_ref, *refs):
    blocks, (u0_ref, u1_ref) = refs[:-2], refs[-2:]
    width = u0_ref.shape[1]
    step = step_of(width)
    for at in range(0, width, step):
        cols = slice(at, at + step)
        parts = [block[:, cols] for block in blocks]
        for which, out in ((0, u0_ref), (1, u1_ref)):
            rows = slice(which * NB, (which + 1) * NB)
            hot = jnp.concatenate([hot_ref[rows, a:b] for a, b in spans], axis=1)
            out[:, cols] = dot(hot, list_rows(parts, which)).astype(BF16)


def select(hot, blocks, spans):
    width = blocks[0].shape[1]
    shape = jax.ShapeDtypeStruct((NB, width), BF16)
    slots = sum(b - a for a, b in spans)
    return pl.pallas_call(
        functools.partial(select_kernel, spans),
        in_specs=[VMEM] * (1 + len(blocks)),
        out_specs=[VMEM, VMEM],
        out_shape=[shape, shape],
        compiler_params=PARAMS,
        cost_estimate=pl.CostEstimate(
            flops=2 * 2 * NB * slots * width, bytes_accessed=2**20, transcendentals=0
        ),
        name="select",
    )(hot, *blocks)


def update_kernel(
    start, span, ids, hot_ref, u0_ref, u1_ref, mine_ref, other_ref, l0_ref, l1_ref, lp_ref, fin_ref,
    a_hbm, _, out_hbm, a_ref, out_ref, in_sems, out_sems,
):
    me, col = ids[0], ids[1]
    width = u0_ref.shape[1]
    half = width // 2
    step = step_of(width)
    steps = width // step

    def fetch(k):
        cols = pl.ds(start + k * step, step)
        return pltpu.make_async_copy(a_hbm.at[:, cols], a_ref.at[k], in_sems.at[k])

    def put(k):
        cols = pl.ds(start + k * step, step)
        return pltpu.make_async_copy(out_ref.at[k], out_hbm.at[:, cols], out_sems.at[k])

    for k in range(steps):
        fetch(k).start()
    for k in range(steps):
        at = k * step
        side = at // half
        cols = slice(at, at + step)
        near = slice(at - side * half, at - side * half + step)
        last = jnp.where(me % 2 == side, mine_ref[:, near], other_ref[:, near])
        u0 = u0_ref[:, cols].astype(F32) + dot(hot_ref[:NB, span], list_rows([last], 0))
        u0 = u0.astype(BF16)
        u1 = u1_ref[:, cols].astype(F32) + dot(hot_ref[NB:, span], list_rows([last], 1))
        u1 = (u1 - dot(lp_ref[...], u0)).astype(BF16)
        fetch(k).wait()
        a = (a_ref[k].astype(F32) - dot(l0_ref[...], u0)).astype(BF16)
        out_ref[k] = (a.astype(F32) - dot(l1_ref[...], u1)).astype(BF16)
        if start + at == 0:

            @pl.when(col < 2)
            def _():
                out_ref[k, :, :NB] = fin_ref[...]

        put(k).start()
    for k in range(steps):
        put(k).wait()


def update(ids, hot, span, uppers, mine, other, lefts, lower, fin, matrix, out, start):
    rows_dev, columns = matrix.shape
    width = uppers[0].shape[1]
    step = step_of(width)
    steps = width // step
    aliases = {}
    if out is None:
        out = jnp.zeros((16, 128), BF16)
    else:
        aliases = {11: 0}
    return pl.pallas_call(
        functools.partial(update_kernel, start, slice(*span)),
        in_specs=[SMEM] + [VMEM] * 9 + [ANY, ANY],
        out_specs=ANY,
        out_shape=jax.ShapeDtypeStruct((rows_dev, columns), BF16),
        scratch_shapes=[
            pltpu.VMEM((steps, rows_dev, step), BF16),
            pltpu.VMEM((steps, rows_dev, step), BF16),
            pltpu.SemaphoreType.DMA((steps,)),
            pltpu.SemaphoreType.DMA((steps,)),
        ],
        input_output_aliases=aliases,
        compiler_params=PARAMS,
        cost_estimate=pl.CostEstimate(
            flops=2 * width * NB * (2 * 128 + NB + 2 * rows_dev),
            bytes_accessed=4 * width * rows_dev,
            transcendentals=0,
        ),
        name="update",
    )(ids, hot, *uppers, mine, other, *lefts, lower, fin, matrix, out)


def on_device(matrix, pivots):
    rows_dev, width = matrix.shape
    me = lax.axis_index("prow")
    col = lax.axis_index("pcol")
    ids = jnp.stack([me, col]).astype(jnp.int32)
    even = me % 2 == 0

    def panels(array, near, far, across):
        zero = jnp.where(col == 0, array, jnp.where(col == 1, near, jnp.where(col == 3, far, across)))
        one = jnp.where(col == 1, array, jnp.where(col == 0, near, jnp.where(col == 2, far, across)))
        return zero, one

    def half(array):
        width = array.shape[1] // 2
        return jnp.where(even, array[:, :width], array[:, width:])

    packed = pick(ids, pivots, matrix)
    packed = packed + send(packed, PAIR)
    zb, yb = packed[:, :WZ], packed[:, WZ:]
    n = CHIP

    hot_z, hot_y = maps(ids, pivots, rows_dev)
    t1, r1, hot_z, hot_y = both(send(zb, ALONG_Z), send(yb, ALONG_Y), hot_z, hot_y)

    t2, r2, q1 = both(send(t1, ALONG_Z), send(r1, ALONG_Y), send(r1, PAIR))
    yf = jnp.concatenate([yb, jnp.where(even, r1, q1), r2, jnp.where(even, q1, r1)], axis=0)

    y1 = send(yf, ALONG_Z)
    t3 = send(t2, ALONG_Z)
    own = jnp.concatenate([t1, t2, t3], axis=0)
    t4, oth, y1 = both(send(t3, ALONG_Z), send(own, PAIR), y1)

    def z_blocks(cols):
        own_cols, oth_cols = own[:, cols], oth[:, cols]
        down, up = jnp.where(even, own_cols, oth_cols), jnp.where(even, oth_cols, own_cols)
        order = [zb[:, cols], down, t4[:, cols], up[2 * n :], up[n : 2 * n], up[:n]]
        return jnp.concatenate(order, axis=0)

    v0 = z_blocks(slice(0, NB))
    zf = z_blocks(slice(0, WZ))
    v1, v2 = both(send(v0, ALONG_Y), send(v0, TWICE_Y))
    z1 = send(after(zf, v1), ALONG_Y)
    w1 = send(v1, PAIR)
    k = ZN * SLOTS
    entries = select(hot_z, [v0, v1, v2, w1], [(i * k, (i + 1) * k) for i in range(4)])
    panel = after(matrix[:, :NB], v1)
    near, far = over(panel, NEAR), over(panel, FAR)
    y2, o1, near, far, *entries = both(
        send(y1, ALONG_Z), send(y1, PAIR), near, far, *entries
    )

    part = jnp.where(even, entries[0], entries[1])
    part = panels(part, over(part, NEAR), over(part, FAR), over(part, SKIP))
    part = jnp.concatenate(part, axis=1)
    across = over(far, ACROSS)
    y3, z1, o2, part, across = both(send(y2, ALONG_Z), z1, send(y2, PAIR), part, across)
    pan0, pan1 = panels(panel, near, far, across)

    rest = send(part, PAIR)
    uppers = jnp.concatenate([jnp.where(even, part, rest), jnp.where(even, rest, part)], axis=0)
    uppers = [uppers[:, :NB], uppers[:, NB:]]
    left0, left1, lower, fin = factor(ids, pivots, uppers, pan0, pan1)
    p1, o3 = send(z1, PAIR), send(y3, PAIR)
    uz = select(hot_z, [zf, z1, p1], [(0, k), (k, 2 * k), (3 * k, 4 * k)])
    n = YN * SLOTS
    spans = [(i * n, (i + 1) * n) for i in (0, 1, 2, 3, 5, 6, 7)]
    uy = select(hot_y, [yf, y1, y2, y3, o3, o2, o1], spans)
    z2, y4, left0, *us = both(
        send(half(z1), ALONG_Y), send(half(y3), ALONG_Z), left0, *uz, *uy
    )
    uz, uy = us[:2], us[2:]

    lefts = (left0, left1)
    p2, o4 = send(z2, PAIR), send(y4, PAIR)
    out = update(ids, hot_z, (2 * k, 3 * k), uz, z2, p2, lefts, lower, fin, matrix, None, 0)
    return update(ids, hot_y, (4 * n, 5 * n), uy, y4, o4, lefts, lower, fin, matrix, out, WZ)


def solution(mesh):
    return jax.shard_map(
        on_device,
        mesh=mesh,
        in_specs=(P("prow", "pcol"), P()),
        out_specs=P("prow", "pcol"),
        check_vma=False,
    )
```

```python
import functools
import jax
import jax.numpy as jnp
from jax import lax
from jax.experimental import pallas as pl
from jax.experimental.pallas import tpu as pltpu
from jax.sharding import PartitionSpec as P

NB = 256
NEWTON = 3
ZN, YN = 8, 4
CAP = 8
SLOTS = 2 * CAP
CHIP = 2 * SLOTS
WZ = 2048
F32 = jnp.float32
BF16 = jnp.bfloat16
VMEM = pl.BlockSpec(memory_space=pltpu.VMEM)
SMEM = pl.BlockSpec(memory_space=pltpu.SMEM)
ANY = pl.BlockSpec(memory_space=pl.ANY)
HBM = pl.BlockSpec(memory_space=pltpu.HBM)
PARAMS = pltpu.CompilerParams(vmem_limit_bytes=16 * 2**20)


def moves(dz, dy):
    pairs = []
    for z in range(ZN):
        for y in range(YN):
            for core in range(2):
                sign = 1 - 2 * core
                there = ((z + sign * dz) % ZN) * YN + (y + sign * dy) % YN
                pairs.append(((z * YN + y) * 2 + core, there * 2 + core))
    return pairs


ALONG_Z = moves(1, 0)
ALONG_Y = moves(0, 1)
TWICE_Y = moves(0, 2)
PAIR = [(i, i ^ 1) for i in range(2 * ZN * YN)]


NEAR = [(0, 1), (1, 0)]
FAR = [(0, 3), (1, 2)]
SKIP = [(0, 2), (1, 3)]
ACROSS = [(2, 3), (3, 2)]


def over(array, pairs):
    return lax.ppermute(array, "pcol", pairs)


def send(array, pairs):
    return lax.ppermute(array, "prow", pairs)


def after(array, *others):
    return lax.optimization_barrier((array, *others))[0]


def both(*arrays):
    return lax.optimization_barrier(arrays)


def iota(shape, dim):
    return lax.broadcasted_iota(jnp.int32, shape, dim)


def to_column(row):
    n = row.shape[1]
    eye = iota((n, n), 0) == iota((n, n), 1)
    return jnp.sum(jnp.where(eye, row, 0.0), axis=1, keepdims=True)


def slot_column(piv_row, rows_dev):
    n = piv_row.shape[1]
    owner_row = lax.div(piv_row, jnp.int32(rows_dev)).astype(F32)
    owner_col = to_column(owner_row)
    before = iota((n, n), 1) < iota((n, n), 0)
    rank = jnp.sum(jnp.where(before & (owner_row == owner_col), 1.0, 0.0), axis=1, keepdims=True)
    return owner_col * CAP + rank


def chip_slots(me, order):
    n = ZN * YN * SLOTS
    pos = iota((1, n), 1)
    block = pos // SLOTS
    chip = me // 2
    z, y = chip // YN, chip % YN
    sign = 2 * (me % 2) - 1
    if order == "z first":
        zz = (z - block % ZN) & (ZN - 1)
        yy = (y + sign * (block // ZN)) & (YN - 1)
    else:
        yy = (y - block % YN) & (YN - 1)
        zz = (z + sign * (block // YN)) & (ZN - 1)
    return ((zz * YN + yy) * SLOTS + pos % SLOTS).astype(F32)


def is_pivot(piv_row, me, rows_dev):
    local = piv_row - me * rows_dev
    hit = iota((rows_dev, piv_row.shape[1]), 0) == local
    return jnp.max(jnp.where(hit, 1.0, 0.0), axis=1, keepdims=True) > 0.5


def list_rows(blocks, which):
    parts = []
    for block in blocks:
        rows, width = block.shape
        chips = rows // CHIP
        parts.append(block.reshape(chips, 2, SLOTS, width)[:, which].reshape(chips * SLOTS, width))
    return jnp.concatenate(parts, axis=0) if len(parts) > 1 else parts[0]


def dot(a, b):
    return jnp.dot(a, b, preferred_element_type=F32)


def pieces(b):
    high = b.astype(BF16)
    rest = b - high.astype(F32)
    middle = rest.astype(BF16)
    return high, middle, (rest - middle.astype(F32)).astype(BF16)


def dot_exact(a, parts):
    high, middle, low = parts
    return dot(a, high) + (dot(a, middle) + dot(a, low))


def pick_kernel(chunk, ids, piv_ref, a_hbm, out_ref, a_ref, sems):
    me = ids[0]
    chunks, rows_dev, _ = a_ref.shape

    def fetch(k):
        return pltpu.make_async_copy(
            a_hbm.at[:, pl.ds(k * chunk, chunk)], a_ref.at[k], sems.at[k]
        )

    for k in range(chunks):
        fetch(k).start()
    hots = []
    for which in range(2):
        piv_row = piv_ref[which : which + 1, :]
        n = piv_row.shape[1]
        owner_row = lax.div(piv_row, jnp.int32(rows_dev)).astype(F32)
        owner_col = to_column(owner_row)
        before = iota((n, n), 0) < iota((n, n), 1)
        rank = jnp.sum(jnp.where(before & (owner_row == owner_col), 1.0, 0.0), axis=0, keepdims=True)
        slot = rank + ((me % 2) * CAP).astype(F32)
        mine = owner_row == me.astype(F32)
        place = mine & (iota((SLOTS, n), 0).astype(F32) == slot)
        local = to_column((piv_row - me * rows_dev).astype(F32))
        row = local == iota((n, rows_dev), 1).astype(F32)
        hot = dot(jnp.where(place, 1.0, 0.0).astype(BF16), jnp.where(row, 1.0, 0.0).astype(BF16))
        hots.append(hot)
    hot = jnp.concatenate(hots, axis=0).astype(BF16)
    for k in range(chunks):
        fetch(k).wait()
        out_ref[:, k * chunk : (k + 1) * chunk] = dot(hot, a_ref[k]).astype(BF16)


def pick(ids, pivots, matrix):
    rows_dev, width = matrix.shape
    chunk = 1024
    chunks = width // chunk
    return pl.pallas_call(
        functools.partial(pick_kernel, chunk),
        in_specs=[SMEM, VMEM, HBM],
        out_specs=VMEM,
        out_shape=jax.ShapeDtypeStruct((CHIP, width), BF16),
        scratch_shapes=[
            pltpu.VMEM((chunks, rows_dev, chunk), BF16),
            pltpu.SemaphoreType.DMA((chunks,)),
        ],
        compiler_params=PARAMS,
        cost_estimate=pl.CostEstimate(
            flops=2 * CHIP * rows_dev * width, bytes_accessed=4 * rows_dev * width, transcendentals=0
        ),
        name="pick",
    )(ids, pivots, pltpu.with_memory_space_constraint(matrix, pltpu.HBM))


def maps_kernel(rows_dev, ids, piv_ref, *out_refs):
    me = ids[0]
    for which in range(2):
        slots = slot_column(piv_ref[which : which + 1, :], rows_dev)
        rows = slice(which * NB, (which + 1) * NB)
        for order, out in zip(("z first", "y first"), out_refs):
            out[rows, :] = jnp.where(slots == chip_slots(me, order), 1.0, 0.0).astype(BF16)


def maps(ids, pivots, rows_dev):
    shape = jax.ShapeDtypeStruct((2 * NB, ZN * YN * SLOTS), BF16)
    return pl.pallas_call(
        functools.partial(maps_kernel, rows_dev),
        in_specs=[SMEM, VMEM],
        out_specs=[VMEM] * 2,
        out_shape=[shape] * 2,
        cost_estimate=pl.CostEstimate(flops=2**30, bytes_accessed=2**22, transcendentals=0),
        name="maps",
    )(ids, pivots)


def inverse(block):
    n = block.shape[0]
    wide = block.astype(F32)
    eye = iota((n, n), 0) == iota((n, n), 1)
    diagonal_row = jnp.sum(jnp.where(eye, wide, 0.0), axis=0, keepdims=True)
    diagonal_col = jnp.sum(jnp.where(eye, wide, 0.0), axis=1, keepdims=True)
    twice = jnp.where(eye, 2.0, 0.0)
    guess = (1.0 / diagonal_col) * (twice - wide * (1.0 / diagonal_row))
    for step in range(NEWTON - 1):
        parts = pieces(guess)
        rest_high, rest_low, _ = pieces(0.5 * twice - dot_exact(block, parts))
        change = dot(parts[0], rest_low) + dot(parts[1], rest_high)
        guess = guess + (dot(parts[0], rest_high) + change)
    return guess


def factor_kernel(ids, piv_ref, s0_ref, s1_ref, pan0_ref, pan1_ref, l0_ref, l1_ref, lp_ref, fin_ref):
    me, col = ids[0], ids[1]
    rows_dev = pan0_ref.shape[0]
    upper01 = s1_ref[:NB, :]
    inv0 = pieces(inverse(s0_ref[:NB, :]))
    lower = dot_exact(s0_ref[NB:, :], inv0).astype(BF16)
    lp_ref[...] = lower
    block1 = (s1_ref[NB:, :].astype(F32) - dot(lower, upper01)).astype(BF16)
    inv1 = pieces(inverse(block1))
    live0 = jnp.logical_not(is_pivot(piv_ref[0:1, :], me, rows_dev))
    live1 = live0 & jnp.logical_not(is_pivot(piv_ref[1:2, :], me, rows_dev))
    pan0 = pan0_ref[...]
    left0 = jnp.where(live0, dot_exact(pan0, inv0), 0.0).astype(BF16)
    l0_ref[...] = left0
    pan1 = (pan1_ref[...].astype(F32) - dot(left0, upper01)).astype(BF16)
    left1 = jnp.where(live1, dot_exact(pan1, inv1), 0.0).astype(BF16)
    l1_ref[...] = left1
    fin0 = jnp.where(live0, left0.astype(F32), pan0.astype(F32))
    fin1 = jnp.where(live1, left1.astype(F32), pan1.astype(F32))
    fin_ref[...] = jnp.where(col == 0, fin0, fin1).astype(BF16)


def factor(ids, pivots, uppers, pan0, pan1):
    rows_dev = pan0.shape[0]
    left = jax.ShapeDtypeStruct((rows_dev, NB), BF16)
    return pl.pallas_call(
        factor_kernel,
        in_specs=[SMEM] + [VMEM] * 5,
        out_specs=[VMEM] * 4,
        out_shape=[left, left, jax.ShapeDtypeStruct((NB, NB), BF16), left],
        compiler_params=PARAMS,
        cost_estimate=pl.CostEstimate(
            flops=2 * 3 * 64 * NB**3, bytes_accessed=4 * 2**20, transcendentals=0
        ),
        name="factor",
    )(ids, pivots, *uppers, pan0, pan1)


def assemble_kernel(ids, near_ref, own_ref, other_ref, far_ref, all_ref, first_ref):
    even = ids[0] % 2 == 0
    n = CHIP
    own, other = own_ref[...], other_ref[...]
    down, up = jnp.where(even, own, other), jnp.where(even, other, own)
    order = [near_ref[...], down, far_ref[...], up[2 * n :], up[n : 2 * n], up[:n]]
    blocks = jnp.concatenate(order, axis=0)
    all_ref[...] = blocks
    first_ref[...] = blocks[:, :NB]


def assemble(ids, near, own, other, far):
    width = near.shape[1]
    return pl.pallas_call(
        assemble_kernel,
        in_specs=[SMEM] + [VMEM] * 4,
        out_specs=[VMEM, VMEM],
        out_shape=[
            jax.ShapeDtypeStruct((ZN * CHIP, width), BF16),
            jax.ShapeDtypeStruct((ZN * CHIP, NB), BF16),
        ],
        compiler_params=PARAMS,
        cost_estimate=pl.CostEstimate(flops=2**20, bytes_accessed=2**20, transcendentals=0),
        name="assemble",
    )(ids, near, own, other, far)


def step_of(width):
    if width < 512:
        return width
    return 640 if width % 1280 == 0 else 512


def select_kernel(spans, hot_ref, *refs):
    blocks, (u0_ref, u1_ref) = refs[:-2], refs[-2:]
    width = u0_ref.shape[1]
    step = step_of(width)
    for at in range(0, width, step):
        cols = slice(at, at + step)
        parts = [block[:, cols] for block in blocks]
        for which, out in ((0, u0_ref), (1, u1_ref)):
            rows = slice(which * NB, (which + 1) * NB)
            hot = jnp.concatenate([hot_ref[rows, a:b] for a, b in spans], axis=1)
            out[:, cols] = dot(hot, list_rows(parts, which)).astype(BF16)


def select(hot, blocks, spans):
    width = blocks[0].shape[1]
    shape = jax.ShapeDtypeStruct((NB, width), BF16)
    slots = sum(b - a for a, b in spans)
    return pl.pallas_call(
        functools.partial(select_kernel, spans),
        in_specs=[VMEM] * (1 + len(blocks)),
        out_specs=[VMEM, VMEM],
        out_shape=[shape, shape],
        compiler_params=PARAMS,
        cost_estimate=pl.CostEstimate(
            flops=2 * 2 * NB * slots * width, bytes_accessed=2**20, transcendentals=0
        ),
        name="select",
    )(hot, *blocks)


def update_kernel(
    spans, ids, hotz_ref, hoty_ref, uz0, uz1, z_mine, z_other, uy0, uy1, y_mine, y_other,
    l0_ref, l1_ref, lp_ref, fin_ref, a_ref, out_hbm, out_ref, sems,
):
    me, col = ids[0], ids[1]
    puts = []
    start = 0
    for span, hot_ref, u0_ref, u1_ref, mine_ref, other_ref in (
        (spans[0], hotz_ref, uz0, uz1, z_mine, z_other),
        (spans[1], hoty_ref, uy0, uy1, y_mine, y_other),
    ):
        width = u0_ref.shape[1]
        half = width // 2
        step = step_of(width)
        for at in range(0, width, step):
            side = at // half
            cols = slice(at, at + step)
            near = slice(at - side * half, at - side * half + step)
            whole = slice(start + at, start + at + step)
            last = jnp.where(me % 2 == side, mine_ref[:, near], other_ref[:, near])
            u0 = u0_ref[:, cols].astype(F32) + dot(hot_ref[:NB, span], list_rows([last], 0))
            u0 = u0.astype(BF16)
            u1 = u1_ref[:, cols].astype(F32) + dot(hot_ref[NB:, span], list_rows([last], 1))
            u1 = (u1 - dot(lp_ref[...], u0)).astype(BF16)
            a = (a_ref[:, whole].astype(F32) - dot(l0_ref[...], u0)).astype(BF16)
            out_ref[:, whole] = (a.astype(F32) - dot(l1_ref[...], u1)).astype(BF16)
            if start + at == 0:

                @pl.when(col < 2)
                def _():
                    out_ref[:, :NB] = fin_ref[...]

            put = pltpu.make_async_copy(
                out_ref.at[:, whole], out_hbm.at[:, whole], sems.at[len(puts)]
            )
            put.start()
            puts.append(put)
        start += width
    for put in puts:
        put.wait()


def update(ids, hots, spans, z_parts, y_parts, lefts, lower, fin, matrix):
    rows_dev, columns = matrix.shape
    steps = sum(parts[0].shape[1] // step_of(parts[0].shape[1]) for parts in (z_parts, y_parts))
    return pl.pallas_call(
        functools.partial(update_kernel, [slice(*span) for span in spans]),
        in_specs=[SMEM] + [VMEM] * 15,
        out_specs=ANY,
        out_shape=jax.ShapeDtypeStruct((rows_dev, columns), BF16),
        scratch_shapes=[pltpu.VMEM((rows_dev, columns), BF16), pltpu.SemaphoreType.DMA((steps,))],
        compiler_params=PARAMS,
        cost_estimate=pl.CostEstimate(
            flops=2 * columns * NB * (2 * 128 + NB + 2 * rows_dev),
            bytes_accessed=4 * columns * rows_dev,
            transcendentals=0,
        ),
        name="update",
    )(ids, *hots, *z_parts, *y_parts, *lefts, lower, fin, matrix)


def on_device(matrix, pivots):
    rows_dev, width = matrix.shape
    me = lax.axis_index("prow")
    col = lax.axis_index("pcol")
    ids = jnp.stack([me, col]).astype(jnp.int32)
    even = me % 2 == 0

    def panels(array, near, far, across):
        zero = jnp.where(col == 0, array, jnp.where(col == 1, near, jnp.where(col == 3, far, across)))
        one = jnp.where(col == 1, array, jnp.where(col == 0, near, jnp.where(col == 2, far, across)))
        return zero, one

    def half(array):
        width = array.shape[1] // 2
        return jnp.where(even, array[:, :width], array[:, width:])

    packed = pick(ids, pivots, matrix)
    packed = packed + send(packed, PAIR)
    zb, yb = packed[:, :WZ], packed[:, WZ:]
    n = CHIP

    hot_z, hot_y = maps(ids, pivots, rows_dev)
    t1, r1, hot_z, hot_y = both(send(zb, ALONG_Z), send(yb, ALONG_Y), hot_z, hot_y)

    panel = after(matrix[:, :NB], t1)
    near, far = over(panel, NEAR), over(panel, FAR)
    t2, r2, q1 = both(send(t1, ALONG_Z), send(r1, ALONG_Y), send(r1, PAIR))
    yf = jnp.concatenate([yb, jnp.where(even, r1, q1), r2, jnp.where(even, q1, r1)], axis=0)

    y1 = send(yf, ALONG_Z)
    t3, near, far = both(send(t2, ALONG_Z), near, far)
    own = jnp.concatenate([t1, t2, t3], axis=0)
    t4, oth, y1 = both(send(t3, ALONG_Z), send(own, PAIR), y1)

    zf, v0 = assemble(ids, zb, own, oth, t4)
    across = over(far, ACROSS)
    v1, v2, across = both(send(v0, ALONG_Y), send(half(v0), TWICE_Y), across)
    z1 = send(after(zf, v1), ALONG_Y)
    w = send(jnp.concatenate([v1, v2], axis=1), PAIR)
    w1, w2 = w[:, :NB], w[:, NB:]
    opposite = jnp.concatenate([jnp.where(even, v2, w2), jnp.where(even, w2, v2)], axis=1)
    k = ZN * SLOTS
    entries = select(hot_z, [v0, v1, opposite, w1], [(i * k, (i + 1) * k) for i in range(4)])
    y2, o1, *entries = both(send(y1, ALONG_Z), send(y1, PAIR), *entries)
    pan0, pan1 = panels(panel, near, far, across)

    part = jnp.where(even, entries[0], entries[1])
    part = panels(part, over(part, NEAR), over(part, FAR), over(part, SKIP))
    part = jnp.concatenate(part, axis=1)
    y3, z1, o2, part = both(send(y2, ALONG_Z), z1, send(y2, PAIR), part)

    rest = send(part, PAIR)
    uppers = jnp.concatenate([jnp.where(even, part, rest), jnp.where(even, rest, part)], axis=0)
    uppers = [uppers[:, :NB], uppers[:, NB:]]
    left0, left1, lower, fin = factor(ids, pivots, uppers, pan0, pan1)
    p1, o3 = send(z1, PAIR), send(y3, PAIR)
    uz = select(hot_z, [zf, z1, p1], [(0, k), (k, 2 * k), (3 * k, 4 * k)])
    n = YN * SLOTS
    spans = [(i * n, (i + 1) * n) for i in (0, 1, 2, 3, 5, 6, 7)]
    uy = select(hot_y, [yf, y1, y2, y3, o3, o2, o1], spans)
    z2, y4, left0, *us = both(
        send(half(z1), ALONG_Y), send(half(y3), ALONG_Z), left0, *uz, *uy
    )
    p2, o4 = send(z2, PAIR), send(y4, PAIR)
    spans = ((2 * k, 3 * k), (4 * n, 5 * n))
    z_parts, y_parts = (*us[:2], z2, p2), (*us[2:], y4, o4)
    return update(
        ids, (hot_z, hot_y), spans, z_parts, y_parts, (left0, left1), lower, fin, matrix
    )


def solution(mesh):
    return jax.shard_map(
        on_device,
        mesh=mesh,
        in_specs=(P("prow", "pcol"), P()),
        out_specs=P("prow", "pcol"),
        check_vma=False,
    )
```

```python
import functools
import jax
import jax.numpy as jnp
from jax import lax
from jax.experimental import pallas as pl
from jax.experimental.pallas import tpu as pltpu
from jax.sharding import PartitionSpec as P

NB = 256
NEWTON = 3
ZN, YN = 8, 4
CAP = 8
SLOTS = 2 * CAP
CHIP = 2 * SLOTS
WZ = 2048
F32 = jnp.float32
BF16 = jnp.bfloat16
VMEM = pl.BlockSpec(memory_space=pltpu.VMEM)
SMEM = pl.BlockSpec(memory_space=pltpu.SMEM)
ANY = pl.BlockSpec(memory_space=pl.ANY)
HBM = pl.BlockSpec(memory_space=pltpu.HBM)
PARAMS = pltpu.CompilerParams(vmem_limit_bytes=16 * 2**20)


def moves(dz, dy):
    pairs = []
    for z in range(ZN):
        for y in range(YN):
            for core in range(2):
                sign = 1 - 2 * core
                there = ((z + sign * dz) % ZN) * YN + (y + sign * dy) % YN
                pairs.append(((z * YN + y) * 2 + core, there * 2 + core))
    return pairs


ALONG_Z = moves(1, 0)
ALONG_Y = moves(0, 1)
TWICE_Y = moves(0, 2)
PAIR = [(i, i ^ 1) for i in range(2 * ZN * YN)]


NEAR = [(0, 1), (1, 0), (2, 3), (3, 2)]
FAR = [(0, 3), (1, 2), (2, 1), (3, 0)]
SKIP = [(0, 2), (1, 3), (2, 0), (3, 1)]


def over(array, pairs):
    return lax.ppermute(array, "pcol", pairs)


def send(array, pairs):
    return lax.ppermute(array, "prow", pairs)


def after(array, *others):
    return lax.optimization_barrier((array, *others))[0]


def both(*arrays):
    return lax.optimization_barrier(arrays)


def iota(shape, dim):
    return lax.broadcasted_iota(jnp.int32, shape, dim)


def to_column(row):
    n = row.shape[1]
    eye = iota((n, n), 0) == iota((n, n), 1)
    return jnp.sum(jnp.where(eye, row, 0.0), axis=1, keepdims=True)


def slot_column(piv_row, rows_dev):
    n = piv_row.shape[1]
    owner_row = lax.div(piv_row, jnp.int32(rows_dev)).astype(F32)
    owner_col = to_column(owner_row)
    before = iota((n, n), 1) < iota((n, n), 0)
    rank = jnp.sum(jnp.where(before & (owner_row == owner_col), 1.0, 0.0), axis=1, keepdims=True)
    return owner_col * CAP + rank


def chip_slots(me, order):
    n = ZN * YN * SLOTS
    pos = iota((1, n), 1)
    block = pos // SLOTS
    chip = me // 2
    z, y = chip // YN, chip % YN
    sign = 2 * (me % 2) - 1
    if order == "z first":
        zz = (z - block % ZN) & (ZN - 1)
        yy = (y + sign * (block // ZN)) & (YN - 1)
    else:
        yy = (y - block % YN) & (YN - 1)
        zz = (z + sign * (block // YN)) & (ZN - 1)
    return ((zz * YN + yy) * SLOTS + pos % SLOTS).astype(F32)


def is_pivot(piv_row, me, rows_dev):
    local = piv_row - me * rows_dev
    hit = iota((rows_dev, piv_row.shape[1]), 0) == local
    return jnp.max(jnp.where(hit, 1.0, 0.0), axis=1, keepdims=True) > 0.5


def list_rows(blocks, which):
    parts = []
    for block in blocks:
        rows, width = block.shape
        chips = rows // CHIP
        parts.append(block.reshape(chips, 2, SLOTS, width)[:, which].reshape(chips * SLOTS, width))
    return jnp.concatenate(parts, axis=0) if len(parts) > 1 else parts[0]


def dot(a, b):
    return jnp.dot(a, b, preferred_element_type=F32)


def pieces(b):
    high = b.astype(BF16)
    rest = b - high.astype(F32)
    middle = rest.astype(BF16)
    return high, middle, (rest - middle.astype(F32)).astype(BF16)


def dot_exact(a, parts):
    high, middle, low = parts
    return dot(a, high) + (dot(a, middle) + dot(a, low))


def pick_kernel(chunk, ids, piv_ref, a_hbm, out_ref, a_ref, sems):
    me = ids[0]
    chunks, rows_dev, _ = a_ref.shape

    def fetch(k):
        return pltpu.make_async_copy(
            a_hbm.at[:, pl.ds(k * chunk, chunk)], a_ref.at[k], sems.at[k]
        )

    for k in range(chunks):
        fetch(k).start()
    hots = []
    for which in range(2):
        piv_row = piv_ref[which : which + 1, :]
        n = piv_row.shape[1]
        owner_row = lax.div(piv_row, jnp.int32(rows_dev)).astype(F32)
        owner_col = to_column(owner_row)
        before = iota((n, n), 0) < iota((n, n), 1)
        rank = jnp.sum(jnp.where(before & (owner_row == owner_col), 1.0, 0.0), axis=0, keepdims=True)
        slot = rank + ((me % 2) * CAP).astype(F32)
        mine = owner_row == me.astype(F32)
        place = mine & (iota((SLOTS, n), 0).astype(F32) == slot)
        local = to_column((piv_row - me * rows_dev).astype(F32))
        row = local == iota((n, rows_dev), 1).astype(F32)
        hot = dot(jnp.where(place, 1.0, 0.0).astype(BF16), jnp.where(row, 1.0, 0.0).astype(BF16))
        hots.append(hot)
    hot = jnp.concatenate(hots, axis=0).astype(BF16)
    for k in range(chunks):
        fetch(k).wait()
        out_ref[:, k * chunk : (k + 1) * chunk] = dot(hot, a_ref[k]).astype(BF16)


def pick(ids, pivots, matrix):
    rows_dev, width = matrix.shape
    chunk = 1024
    chunks = width // chunk
    return pl.pallas_call(
        functools.partial(pick_kernel, chunk),
        in_specs=[SMEM, VMEM, HBM],
        out_specs=VMEM,
        out_shape=jax.ShapeDtypeStruct((CHIP, width), BF16),
        scratch_shapes=[
            pltpu.VMEM((chunks, rows_dev, chunk), BF16),
            pltpu.SemaphoreType.DMA((chunks,)),
        ],
        compiler_params=PARAMS,
        cost_estimate=pl.CostEstimate(
            flops=2 * CHIP * rows_dev * width, bytes_accessed=4 * rows_dev * width, transcendentals=0
        ),
        name="pick",
    )(ids, pivots, pltpu.with_memory_space_constraint(matrix, pltpu.HBM))


def maps_kernel(rows_dev, ids, piv_ref, *out_refs):
    me = ids[0]
    for which in range(2):
        slots = slot_column(piv_ref[which : which + 1, :], rows_dev)
        rows = slice(which * NB, (which + 1) * NB)
        for order, out in zip(("z first", "y first"), out_refs):
            out[rows, :] = jnp.where(slots == chip_slots(me, order), 1.0, 0.0).astype(BF16)


def maps(ids, pivots, rows_dev):
    shape = jax.ShapeDtypeStruct((2 * NB, ZN * YN * SLOTS), BF16)
    return pl.pallas_call(
        functools.partial(maps_kernel, rows_dev),
        in_specs=[SMEM, VMEM],
        out_specs=[VMEM] * 2,
        out_shape=[shape] * 2,
        cost_estimate=pl.CostEstimate(flops=2**30, bytes_accessed=2**22, transcendentals=0),
        name="maps",
    )(ids, pivots)


def inverse(block):
    n = block.shape[0]
    wide = block.astype(F32)
    eye = iota((n, n), 0) == iota((n, n), 1)
    diagonal_row = jnp.sum(jnp.where(eye, wide, 0.0), axis=0, keepdims=True)
    diagonal_col = jnp.sum(jnp.where(eye, wide, 0.0), axis=1, keepdims=True)
    twice = jnp.where(eye, 2.0, 0.0)
    guess = (1.0 / diagonal_col) * (twice - wide * (1.0 / diagonal_row))
    for step in range(NEWTON - 1):
        parts = pieces(guess)
        rest_high, rest_low, _ = pieces(0.5 * twice - dot_exact(block, parts))
        change = dot(parts[0], rest_low) + dot(parts[1], rest_high)
        guess = guess + (dot(parts[0], rest_high) + change)
    return guess


def factor_kernel(ids, piv_ref, s0_ref, s1_ref, pan0_ref, pan1_ref, l0_ref, l1_ref, lp_ref, fin_ref):
    me, col = ids[0], ids[1]
    rows_dev = pan0_ref.shape[0]
    upper01 = s1_ref[:NB, :]
    inv0 = pieces(inverse(s0_ref[:NB, :]))
    lower = dot_exact(s0_ref[NB:, :], inv0).astype(BF16)
    lp_ref[...] = lower
    block1 = (s1_ref[NB:, :].astype(F32) - dot(lower, upper01)).astype(BF16)
    inv1 = pieces(inverse(block1))
    live0 = jnp.logical_not(is_pivot(piv_ref[0:1, :], me, rows_dev))
    live1 = live0 & jnp.logical_not(is_pivot(piv_ref[1:2, :], me, rows_dev))
    pan0 = pan0_ref[...]
    left0 = jnp.where(live0, dot_exact(pan0, inv0), 0.0).astype(BF16)
    l0_ref[...] = left0
    pan1 = (pan1_ref[...].astype(F32) - dot(left0, upper01)).astype(BF16)
    left1 = jnp.where(live1, dot_exact(pan1, inv1), 0.0).astype(BF16)
    l1_ref[...] = left1
    fin0 = jnp.where(live0, left0.astype(F32), pan0.astype(F32))
    fin1 = jnp.where(live1, left1.astype(F32), pan1.astype(F32))
    fin_ref[...] = jnp.where(col == 0, fin0, fin1).astype(BF16)


def factor(ids, pivots, uppers, pan0, pan1):
    rows_dev = pan0.shape[0]
    left = jax.ShapeDtypeStruct((rows_dev, NB), BF16)
    return pl.pallas_call(
        factor_kernel,
        in_specs=[SMEM] + [VMEM] * 5,
        out_specs=[VMEM] * 4,
        out_shape=[left, left, jax.ShapeDtypeStruct((NB, NB), BF16), left],
        compiler_params=PARAMS,
        cost_estimate=pl.CostEstimate(
            flops=2 * 3 * 64 * NB**3, bytes_accessed=4 * 2**20, transcendentals=0
        ),
        name="factor",
    )(ids, pivots, *uppers, pan0, pan1)


def assemble_kernel(ids, near_ref, own_ref, other_ref, far_ref, all_ref):
    even = ids[0] % 2 == 0
    n = CHIP
    own, other = own_ref[...], other_ref[...]
    down, up = jnp.where(even, own, other), jnp.where(even, other, own)
    order = [near_ref[...], down, far_ref[...], up[2 * n :], up[n : 2 * n], up[:n]]
    all_ref[...] = jnp.concatenate(order, axis=0)


def assemble(ids, near, own, other, far):
    width = near.shape[1]
    return pl.pallas_call(
        assemble_kernel,
        in_specs=[SMEM] + [VMEM] * 4,
        out_specs=VMEM,
        out_shape=jax.ShapeDtypeStruct((ZN * CHIP, width), BF16),
        compiler_params=PARAMS,
        cost_estimate=pl.CostEstimate(flops=2**20, bytes_accessed=2**20, transcendentals=0),
        name="assemble",
    )(ids, near, own, other, far)


def step_of(width):
    if width < 512:
        return width
    return 640 if width % 1280 == 0 else 512


def select_kernel(spans, hot_ref, *refs):
    blocks, (u0_ref, u1_ref) = refs[:-2], refs[-2:]
    width = u0_ref.shape[1]
    step = step_of(width)
    for at in range(0, width, step):
        cols = slice(at, at + step)
        parts = [block[:, cols] for block in blocks]
        for which, out in ((0, u0_ref), (1, u1_ref)):
            rows = slice(which * NB, (which + 1) * NB)
            hot = jnp.concatenate([hot_ref[rows, a:b] for a, b in spans], axis=1)
            out[:, cols] = dot(hot, list_rows(parts, which)).astype(BF16)


def select(hot, blocks, spans):
    width = blocks[0].shape[1]
    shape = jax.ShapeDtypeStruct((NB, width), BF16)
    slots = sum(b - a for a, b in spans)
    return pl.pallas_call(
        functools.partial(select_kernel, spans),
        in_specs=[VMEM] * (1 + len(blocks)),
        out_specs=[VMEM, VMEM],
        out_shape=[shape, shape],
        compiler_params=PARAMS,
        cost_estimate=pl.CostEstimate(
            flops=2 * 2 * NB * slots * width, bytes_accessed=2**20, transcendentals=0
        ),
        name="select",
    )(hot, *blocks)


def update_kernel(
    spans, ids, hotz_ref, hoty_ref, uz0, uz1, z_mine, z_other, uy0, uy1, y_mine, y_other,
    l0_ref, l1_ref, lp_ref, fin_ref, a_ref, out_hbm, out_ref, sems,
):
    me, col = ids[0], ids[1]
    puts = []
    start = 0
    for span, hot_ref, u0_ref, u1_ref, mine_ref, other_ref in (
        (spans[0], hotz_ref, uz0, uz1, z_mine, z_other),
        (spans[1], hoty_ref, uy0, uy1, y_mine, y_other),
    ):
        width = u0_ref.shape[1]
        half = width // 2
        step = step_of(width)
        for at in range(0, width, step):
            side = at // half
            cols = slice(at, at + step)
            near = slice(at - side * half, at - side * half + step)
            whole = slice(start + at, start + at + step)
            last = jnp.where(me % 2 == side, mine_ref[:, near], other_ref[:, near])
            u0 = u0_ref[:, cols].astype(F32) + dot(hot_ref[:NB, span], list_rows([last], 0))
            u0 = u0.astype(BF16)
            u1 = u1_ref[:, cols].astype(F32) + dot(hot_ref[NB:, span], list_rows([last], 1))
            u1 = (u1 - dot(lp_ref[...], u0)).astype(BF16)
            a = (a_ref[:, whole].astype(F32) - dot(l0_ref[...], u0)).astype(BF16)
            out_ref[:, whole] = (a.astype(F32) - dot(l1_ref[...], u1)).astype(BF16)
            if start + at == 0:

                @pl.when(col < 2)
                def _():
                    out_ref[:, :NB] = fin_ref[...]

            put = pltpu.make_async_copy(
                out_ref.at[:, whole], out_hbm.at[:, whole], sems.at[len(puts)]
            )
            put.start()
            puts.append(put)
        start += width
    for put in puts:
        put.wait()


def update(ids, hots, spans, z_parts, y_parts, lefts, lower, fin, matrix):
    rows_dev, columns = matrix.shape
    steps = sum(parts[0].shape[1] // step_of(parts[0].shape[1]) for parts in (z_parts, y_parts))
    return pl.pallas_call(
        functools.partial(update_kernel, [slice(*span) for span in spans]),
        in_specs=[SMEM] + [VMEM] * 15,
        out_specs=ANY,
        out_shape=jax.ShapeDtypeStruct((rows_dev, columns), BF16),
        scratch_shapes=[pltpu.VMEM((rows_dev, columns), BF16), pltpu.SemaphoreType.DMA((steps,))],
        compiler_params=PARAMS,
        cost_estimate=pl.CostEstimate(
            flops=2 * columns * NB * (2 * 128 + NB + 2 * rows_dev),
            bytes_accessed=4 * columns * rows_dev,
            transcendentals=0,
        ),
        name="update",
    )(ids, *hots, *z_parts, *y_parts, *lefts, lower, fin, matrix)


def on_device(matrix, pivots):
    rows_dev, width = matrix.shape
    me = lax.axis_index("prow")
    col = lax.axis_index("pcol")
    ids = jnp.stack([me, col]).astype(jnp.int32)
    even = me % 2 == 0

    def panels(array, near, far, across):
        zero = jnp.where(col == 0, array, jnp.where(col == 1, near, jnp.where(col == 3, far, across)))
        one = jnp.where(col == 1, array, jnp.where(col == 0, near, jnp.where(col == 2, far, across)))
        return zero, one

    def half(array):
        width = array.shape[1] // 2
        return jnp.where(even, array[:, :width], array[:, width:])

    packed = pick(ids, pivots, matrix)
    packed = packed + send(packed, PAIR)
    zb, yb = packed[:, :WZ], packed[:, WZ:]
    n = CHIP

    hot_z, hot_y = maps(ids, pivots, rows_dev)
    t1, r1, hot_z, hot_y = both(send(zb, ALONG_Z), send(yb, ALONG_Y), hot_z, hot_y)

    panel = after(matrix[:, :NB], t1)
    near, far = over(panel, NEAR), over(panel, FAR)
    t2, r2, q1 = both(send(t1, ALONG_Z), send(r1, ALONG_Y), send(r1, PAIR))
    yf = jnp.concatenate([yb, jnp.where(even, r1, q1), r2, jnp.where(even, q1, r1)], axis=0)

    y1 = send(yf, ALONG_Z)
    t3, near, far = both(send(t2, ALONG_Z), near, far)
    own = jnp.concatenate([t1, t2, t3], axis=0)
    t4, oth, y1 = both(send(t3, ALONG_Z), send(own, PAIR), y1)

    own_first, oth_first = own[:, :NB], oth[:, :NB]
    down, up = jnp.where(even, own_first, oth_first), jnp.where(even, oth_first, own_first)
    order = [zb[:, :NB], down, t4[:, :NB], up[2 * n :], up[n : 2 * n], up[:n]]
    v0 = jnp.concatenate(order, axis=0)
    zf = assemble(after(ids, v0), zb, own, oth, t4)
    across = over(far, NEAR)
    v1, v2, across = both(send(v0, ALONG_Y), send(half(v0), TWICE_Y), across)
    z1 = send(after(zf, v1), ALONG_Y)
    w = send(jnp.concatenate([v1, v2], axis=1), PAIR)
    w1, w2 = w[:, :NB], w[:, NB:]
    opposite = jnp.concatenate([jnp.where(even, v2, w2), jnp.where(even, w2, v2)], axis=1)
    k = ZN * SLOTS
    entries = select(hot_z, [v0, v1, opposite, w1], [(i * k, (i + 1) * k) for i in range(4)])
    y2, o1, *entries = both(send(y1, ALONG_Z), send(y1, PAIR), *entries)
    pan0, pan1 = panels(panel, near, far, across)

    part = jnp.where(even, entries[0], entries[1])
    part = panels(part, over(part, NEAR), over(part, FAR), over(part, SKIP))
    part = jnp.concatenate(part, axis=1)
    y3, z1, o2, part = both(send(y2, ALONG_Z), z1, send(y2, PAIR), part)

    rest = send(part, PAIR)
    uppers = jnp.concatenate([jnp.where(even, part, rest), jnp.where(even, rest, part)], axis=0)
    uppers = [uppers[:, :NB], uppers[:, NB:]]
    left0, left1, lower, fin = factor(ids, pivots, uppers, pan0, pan1)
    p1, o3 = send(z1, PAIR), send(y3, PAIR)
    n = YN * SLOTS
    spans = [(i * n, (i + 1) * n) for i in (0, 1, 2, 3, 5, 6, 7)]
    uy = select(hot_y, [yf, y1, y2, y3, o3, o2, o1], spans)
    z2, y4, left0, *uy = both(send(half(z1), ALONG_Y), send(half(y3), ALONG_Z), left0, *uy)
    p2, o4 = send(z2, PAIR), send(y4, PAIR)
    uz = select(after(hot_z, z2), [zf, z1, p1], [(0, k), (k, 2 * k), (3 * k, 4 * k)])
    spans = ((2 * k, 3 * k), (4 * n, 5 * n))
    z_parts, y_parts = (*uz, z2, p2), (*uy, y4, o4)
    return update(
        ids, (hot_z, hot_y), spans, z_parts, y_parts, (left0, left1), lower, fin, matrix
    )


def solution(mesh):
    return jax.shard_map(
        on_device,
        mesh=mesh,
        in_specs=(P("prow", "pcol"), P()),
        out_specs=P("prow", "pcol"),
        check_vma=False,
    )
```

```python
import functools
import jax
import jax.numpy as jnp
from jax import lax
from jax.experimental import pallas as pl
from jax.experimental.pallas import tpu as pltpu
from jax.sharding import PartitionSpec as P

NB = 256
NEWTON = 3
ZN, YN = 8, 4
CAP = 8
SLOTS = 2 * CAP
CHIP = 2 * SLOTS
WZ = 2048
F32 = jnp.float32
BF16 = jnp.bfloat16
VMEM = pl.BlockSpec(memory_space=pltpu.VMEM)
SMEM = pl.BlockSpec(memory_space=pltpu.SMEM)
ANY = pl.BlockSpec(memory_space=pl.ANY)
HBM = pl.BlockSpec(memory_space=pltpu.HBM)
PARAMS = pltpu.CompilerParams(vmem_limit_bytes=16 * 2**20)


def moves(dz, dy):
    pairs = []
    for z in range(ZN):
        for y in range(YN):
            for core in range(2):
                sign = 1 - 2 * core
                there = ((z + sign * dz) % ZN) * YN + (y + sign * dy) % YN
                pairs.append(((z * YN + y) * 2 + core, there * 2 + core))
    return pairs


ALONG_Z = moves(1, 0)
ALONG_Y = moves(0, 1)
TWICE_Y = moves(0, 2)
PAIR = [(i, i ^ 1) for i in range(2 * ZN * YN)]


NEAR = [(0, 1), (1, 0), (2, 3), (3, 2)]
FAR = [(0, 3), (1, 2), (2, 1), (3, 0)]
SKIP = [(0, 2), (1, 3), (2, 0), (3, 1)]


def over(array, pairs):
    return lax.ppermute(array, "pcol", pairs)


def send(array, pairs):
    return lax.ppermute(array, "prow", pairs)


def after(array, *others):
    return lax.optimization_barrier((array, *others))[0]


def both(*arrays):
    return lax.optimization_barrier(arrays)


def iota(shape, dim):
    return lax.broadcasted_iota(jnp.int32, shape, dim)


def to_column(row):
    n = row.shape[1]
    eye = iota((n, n), 0) == iota((n, n), 1)
    return jnp.sum(jnp.where(eye, row, 0.0), axis=1, keepdims=True)


def slot_column(piv_row, rows_dev):
    n = piv_row.shape[1]
    owner_row = lax.div(piv_row, jnp.int32(rows_dev)).astype(F32)
    owner_col = to_column(owner_row)
    before = iota((n, n), 1) < iota((n, n), 0)
    rank = jnp.sum(jnp.where(before & (owner_row == owner_col), 1.0, 0.0), axis=1, keepdims=True)
    return owner_col * CAP + rank


def chip_slots(me, order):
    n = ZN * YN * SLOTS
    pos = iota((1, n), 1)
    block = pos // SLOTS
    chip = me // 2
    z, y = chip // YN, chip % YN
    sign = 2 * (me % 2) - 1
    if order == "z first":
        zz = (z - block % ZN) & (ZN - 1)
        yy = (y + sign * (block // ZN)) & (YN - 1)
    else:
        yy = (y - block % YN) & (YN - 1)
        zz = (z + sign * (block // YN)) & (ZN - 1)
    return ((zz * YN + yy) * SLOTS + pos % SLOTS).astype(F32)


def is_pivot(piv_row, me, rows_dev):
    local = piv_row - me * rows_dev
    hit = iota((rows_dev, piv_row.shape[1]), 0) == local
    return jnp.max(jnp.where(hit, 1.0, 0.0), axis=1, keepdims=True) > 0.5


def list_rows(blocks, which):
    parts = []
    for block in blocks:
        rows, width = block.shape
        chips = rows // CHIP
        parts.append(block.reshape(chips, 2, SLOTS, width)[:, which].reshape(chips * SLOTS, width))
    return jnp.concatenate(parts, axis=0) if len(parts) > 1 else parts[0]


def dot(a, b):
    return jnp.dot(a, b, preferred_element_type=F32)


def pieces(b):
    high = b.astype(BF16)
    rest = b - high.astype(F32)
    middle = rest.astype(BF16)
    return high, middle, (rest - middle.astype(F32)).astype(BF16)


def dot_exact(a, parts):
    high, middle, low = parts
    return dot(a, high) + (dot(a, middle) + dot(a, low))


def pick_kernel(chunk, ids, piv_ref, a_hbm, out_ref, a_ref, sems):
    me = ids[0]
    chunks, rows_dev, _ = a_ref.shape

    def fetch(k):
        return pltpu.make_async_copy(
            a_hbm.at[:, pl.ds(k * chunk, chunk)], a_ref.at[k], sems.at[k]
        )

    for k in range(chunks):
        fetch(k).start()
    hots = []
    for which in range(2):
        piv_row = piv_ref[which : which + 1, :]
        n = piv_row.shape[1]
        owner_row = lax.div(piv_row, jnp.int32(rows_dev)).astype(F32)
        owner_col = to_column(owner_row)
        before = iota((n, n), 0) < iota((n, n), 1)
        rank = jnp.sum(jnp.where(before & (owner_row == owner_col), 1.0, 0.0), axis=0, keepdims=True)
        slot = rank + ((me % 2) * CAP).astype(F32)
        mine = owner_row == me.astype(F32)
        place = mine & (iota((SLOTS, n), 0).astype(F32) == slot)
        local = to_column((piv_row - me * rows_dev).astype(F32))
        row = local == iota((n, rows_dev), 1).astype(F32)
        hot = dot(jnp.where(place, 1.0, 0.0).astype(BF16), jnp.where(row, 1.0, 0.0).astype(BF16))
        hots.append(hot)
    hot = jnp.concatenate(hots, axis=0).astype(BF16)
    for k in range(chunks):
        fetch(k).wait()
        out_ref[:, k * chunk : (k + 1) * chunk] = dot(hot, a_ref[k]).astype(BF16)


def pick(ids, pivots, matrix):
    rows_dev, width = matrix.shape
    chunk = 1024
    chunks = width // chunk
    return pl.pallas_call(
        functools.partial(pick_kernel, chunk),
        in_specs=[SMEM, VMEM, HBM],
        out_specs=VMEM,
        out_shape=jax.ShapeDtypeStruct((CHIP, width), BF16),
        scratch_shapes=[
            pltpu.VMEM((chunks, rows_dev, chunk), BF16),
            pltpu.SemaphoreType.DMA((chunks,)),
        ],
        compiler_params=PARAMS,
        cost_estimate=pl.CostEstimate(
            flops=2 * CHIP * rows_dev * width, bytes_accessed=4 * rows_dev * width, transcendentals=0
        ),
        name="pick",
    )(ids, pivots, pltpu.with_memory_space_constraint(matrix, pltpu.HBM))


def maps_kernel(rows_dev, ids, piv_ref, *out_refs):
    me = ids[0]
    for which in range(2):
        slots = slot_column(piv_ref[which : which + 1, :], rows_dev)
        rows = slice(which * NB, (which + 1) * NB)
        for order, out in zip(("z first", "y first"), out_refs):
            out[rows, :] = jnp.where(slots == chip_slots(me, order), 1.0, 0.0).astype(BF16)


def maps(ids, pivots, rows_dev):
    shape = jax.ShapeDtypeStruct((2 * NB, ZN * YN * SLOTS), BF16)
    return pl.pallas_call(
        functools.partial(maps_kernel, rows_dev),
        in_specs=[SMEM, VMEM],
        out_specs=[VMEM] * 2,
        out_shape=[shape] * 2,
        cost_estimate=pl.CostEstimate(flops=2**30, bytes_accessed=2**22, transcendentals=0),
        name="maps",
    )(ids, pivots)


def inverse(block):
    n = block.shape[0]
    wide = block.astype(F32)
    eye = iota((n, n), 0) == iota((n, n), 1)
    diagonal_row = jnp.sum(jnp.where(eye, wide, 0.0), axis=0, keepdims=True)
    diagonal_col = jnp.sum(jnp.where(eye, wide, 0.0), axis=1, keepdims=True)
    twice = jnp.where(eye, 2.0, 0.0)
    guess = (1.0 / diagonal_col) * (twice - wide * (1.0 / diagonal_row))
    for step in range(NEWTON - 1):
        parts = pieces(guess)
        rest_high, rest_low, _ = pieces(0.5 * twice - dot_exact(block, parts))
        change = dot(parts[0], rest_low) + dot(parts[1], rest_high)
        guess = guess + (dot(parts[0], rest_high) + change)
    return guess


def factor_kernel(ids, piv_ref, s0_ref, s1_ref, pan0_ref, pan1_ref, l0_ref, l1_ref, lp_ref, fin_ref):
    me, col = ids[0], ids[1]
    rows_dev = pan0_ref.shape[0]
    upper01 = s1_ref[:NB, :]
    inv0 = pieces(inverse(s0_ref[:NB, :]))
    lower = dot_exact(s0_ref[NB:, :], inv0).astype(BF16)
    lp_ref[...] = lower
    block1 = (s1_ref[NB:, :].astype(F32) - dot(lower, upper01)).astype(BF16)
    inv1 = pieces(inverse(block1))
    live0 = jnp.logical_not(is_pivot(piv_ref[0:1, :], me, rows_dev))
    live1 = live0 & jnp.logical_not(is_pivot(piv_ref[1:2, :], me, rows_dev))
    pan0 = pan0_ref[...]
    left0 = jnp.where(live0, dot_exact(pan0, inv0), 0.0).astype(BF16)
    l0_ref[...] = left0
    pan1 = (pan1_ref[...].astype(F32) - dot(left0, upper01)).astype(BF16)
    left1 = jnp.where(live1, dot_exact(pan1, inv1), 0.0).astype(BF16)
    l1_ref[...] = left1
    fin0 = jnp.where(live0, left0.astype(F32), pan0.astype(F32))
    fin1 = jnp.where(live1, left1.astype(F32), pan1.astype(F32))
    fin_ref[...] = jnp.where(col == 0, fin0, fin1).astype(BF16)


def factor(ids, pivots, uppers, pan0, pan1):
    rows_dev = pan0.shape[0]
    left = jax.ShapeDtypeStruct((rows_dev, NB), BF16)
    return pl.pallas_call(
        factor_kernel,
        in_specs=[SMEM] + [VMEM] * 5,
        out_specs=[VMEM] * 4,
        out_shape=[left, left, jax.ShapeDtypeStruct((NB, NB), BF16), left],
        compiler_params=PARAMS,
        cost_estimate=pl.CostEstimate(
            flops=2 * 3 * 64 * NB**3, bytes_accessed=4 * 2**20, transcendentals=0
        ),
        name="factor",
    )(ids, pivots, *uppers, pan0, pan1)


def assemble_kernel(ids, near_ref, own_ref, other_ref, far_ref, all_ref):
    even = ids[0] % 2 == 0
    n = CHIP
    own, other = own_ref[...], other_ref[...]
    down, up = jnp.where(even, own, other), jnp.where(even, other, own)
    order = [near_ref[...], down, far_ref[...], up[2 * n :], up[n : 2 * n], up[:n]]
    all_ref[...] = jnp.concatenate(order, axis=0)


def assemble(ids, near, own, other, far):
    width = near.shape[1]
    return pl.pallas_call(
        assemble_kernel,
        in_specs=[SMEM] + [VMEM] * 4,
        out_specs=VMEM,
        out_shape=jax.ShapeDtypeStruct((ZN * CHIP, width), BF16),
        compiler_params=PARAMS,
        cost_estimate=pl.CostEstimate(flops=2**20, bytes_accessed=2**20, transcendentals=0),
        name="assemble",
    )(ids, near, own, other, far)


def step_of(width):
    if width < 512:
        return width
    return 640 if width % 1280 == 0 else 512


def select_kernel(spans, hot_ref, *refs):
    refs, outs = refs[:-2], refs[-2:]
    blocks, earlier = refs[: len(spans)], refs[len(spans) :]
    width = outs[0].shape[1]
    step = step_of(width)
    for at in range(0, width, step):
        cols = slice(at, at + step)
        parts = [block[:, cols] for block in blocks]
        for which, out in enumerate(outs):
            rows = slice(which * NB, (which + 1) * NB)
            hot = jnp.concatenate([hot_ref[rows, a:b] for a, b in spans], axis=1)
            found = dot(hot, list_rows(parts, which))
            if earlier:
                found = found + earlier[which][:, cols].astype(F32)
            out[:, cols] = found.astype(BF16)


def select(hot, blocks, spans, earlier=()):
    width = blocks[0].shape[1]
    shape = jax.ShapeDtypeStruct((NB, width), BF16)
    slots = sum(b - a for a, b in spans)
    return pl.pallas_call(
        functools.partial(select_kernel, spans),
        in_specs=[VMEM] * (1 + len(blocks) + len(earlier)),
        out_specs=[VMEM, VMEM],
        out_shape=[shape, shape],
        compiler_params=PARAMS,
        cost_estimate=pl.CostEstimate(
            flops=2 * 2 * NB * slots * width, bytes_accessed=2**20, transcendentals=0
        ),
        name="select",
    )(hot, *blocks, *earlier)


def update_kernel(
    spans, ids, hotz_ref, hoty_ref, uz0, uz1, z_mine, z_other, uy0, uy1, y_mine, y_other,
    l0_ref, l1_ref, lp_ref, fin_ref, a_ref, out_hbm, out_ref, sems,
):
    me, col = ids[0], ids[1]
    puts = []
    start = 0
    for span, hot_ref, u0_ref, u1_ref, mine_ref, other_ref in (
        (spans[0], hotz_ref, uz0, uz1, z_mine, z_other),
        (spans[1], hoty_ref, uy0, uy1, y_mine, y_other),
    ):
        width = u0_ref.shape[1]
        half = width // 2
        step = step_of(width)
        for at in range(0, width, step):
            side = at // half
            cols = slice(at, at + step)
            near = slice(at - side * half, at - side * half + step)
            whole = slice(start + at, start + at + step)
            last = jnp.where(me % 2 == side, mine_ref[:, near], other_ref[:, near])
            u0 = u0_ref[:, cols].astype(F32) + dot(hot_ref[:NB, span], list_rows([last], 0))
            u0 = u0.astype(BF16)
            u1 = u1_ref[:, cols].astype(F32) + dot(hot_ref[NB:, span], list_rows([last], 1))
            u1 = (u1 - dot(lp_ref[...], u0)).astype(BF16)
            a = (a_ref[:, whole].astype(F32) - dot(l0_ref[...], u0)).astype(BF16)
            out_ref[:, whole] = (a.astype(F32) - dot(l1_ref[...], u1)).astype(BF16)
            if start + at == 0:

                @pl.when(col < 2)
                def _():
                    out_ref[:, :NB] = fin_ref[...]

            put = pltpu.make_async_copy(
                out_ref.at[:, whole], out_hbm.at[:, whole], sems.at[len(puts)]
            )
            put.start()
            puts.append(put)
        start += width
    for put in puts:
        put.wait()


def update(ids, hots, spans, z_parts, y_parts, lefts, lower, fin, matrix):
    rows_dev, columns = matrix.shape
    steps = sum(parts[0].shape[1] // step_of(parts[0].shape[1]) for parts in (z_parts, y_parts))
    return pl.pallas_call(
        functools.partial(update_kernel, [slice(*span) for span in spans]),
        in_specs=[SMEM] + [VMEM] * 15,
        out_specs=ANY,
        out_shape=jax.ShapeDtypeStruct((rows_dev, columns), BF16),
        scratch_shapes=[pltpu.VMEM((rows_dev, columns), BF16), pltpu.SemaphoreType.DMA((steps,))],
        compiler_params=PARAMS,
        cost_estimate=pl.CostEstimate(
            flops=2 * columns * NB * (2 * 128 + NB + 2 * rows_dev),
            bytes_accessed=4 * columns * rows_dev,
            transcendentals=0,
        ),
        name="update",
    )(ids, *hots, *z_parts, *y_parts, *lefts, lower, fin, matrix)


def on_device(matrix, pivots):
    rows_dev, width = matrix.shape
    me = lax.axis_index("prow")
    col = lax.axis_index("pcol")
    ids = jnp.stack([me, col]).astype(jnp.int32)
    even = me % 2 == 0

    def panels(array, near, far, across):
        zero = jnp.where(col == 0, array, jnp.where(col == 1, near, jnp.where(col == 3, far, across)))
        one = jnp.where(col == 1, array, jnp.where(col == 0, near, jnp.where(col == 2, far, across)))
        return zero, one

    def half(array):
        width = array.shape[1] // 2
        return jnp.where(even, array[:, :width], array[:, width:])

    packed = pick(ids, pivots, matrix)
    packed = packed + send(packed, PAIR)
    zb, yb = packed[:, :WZ], packed[:, WZ:]
    n = CHIP

    hot_z, hot_y = maps(ids, pivots, rows_dev)
    t1, r1, hot_z, hot_y = both(send(zb, ALONG_Z), send(yb, ALONG_Y), hot_z, hot_y)

    panel = after(matrix[:, :NB], t1)
    near, far = over(panel, NEAR), over(panel, FAR)
    t2, r2, q1 = both(send(t1, ALONG_Z), send(r1, ALONG_Y), send(r1, PAIR))
    yf = jnp.concatenate([yb, jnp.where(even, r1, q1), r2, jnp.where(even, q1, r1)], axis=0)

    y1 = send(yf, ALONG_Z)
    t3, near, far = both(send(t2, ALONG_Z), near, far)
    own = jnp.concatenate([t1, t2, t3], axis=0)
    t4, oth, y1 = both(send(t3, ALONG_Z), send(own, PAIR), y1)

    own_first, oth_first = own[:, :NB], oth[:, :NB]
    down, up = jnp.where(even, own_first, oth_first), jnp.where(even, oth_first, own_first)
    order = [zb[:, :NB], down, t4[:, :NB], up[2 * n :], up[n : 2 * n], up[:n]]
    v0 = jnp.concatenate(order, axis=0)
    zf = assemble(after(ids, v0), zb, own, oth, t4)
    across = over(far, NEAR)
    v1, v2, across = both(send(v0, ALONG_Y), send(half(v0), TWICE_Y), across)
    z1 = send(after(zf, v1), ALONG_Y)
    w = send(jnp.concatenate([v1, v2], axis=1), PAIR)
    w1, w2 = w[:, :NB], w[:, NB:]
    opposite = jnp.concatenate([jnp.where(even, v2, w2), jnp.where(even, w2, v2)], axis=1)
    k = ZN * SLOTS
    entries = select(hot_z, [v0, v1, opposite, w1], [(i * k, (i + 1) * k) for i in range(4)])
    y2, o1, *entries = both(send(y1, ALONG_Z), send(y1, PAIR), *entries)
    pan0, pan1 = panels(panel, near, far, across)

    part = jnp.where(even, entries[0], entries[1])
    part = panels(part, over(part, NEAR), over(part, FAR), over(part, SKIP))
    part = jnp.concatenate(part, axis=1)
    o2 = send(y2, PAIR)
    n = YN * SLOTS
    spans = [(i * n, (i + 1) * n) for i in (0, 1, 2, 6, 7)]
    uy = select(hot_y, [yf, y1, y2, o2, o1], spans)
    y3, z1, part, *uy = both(send(y2, ALONG_Z), z1, part, *uy)

    rest = send(part, PAIR)
    uppers = jnp.concatenate([jnp.where(even, part, rest), jnp.where(even, rest, part)], axis=0)
    uppers = [uppers[:, :NB], uppers[:, NB:]]
    left0, left1, lower, fin = factor(ids, pivots, uppers, pan0, pan1)
    p1, o3 = send(z1, PAIR), send(y3, PAIR)
    uy = select(hot_y, [y3, o3], [(3 * n, 4 * n), (5 * n, 6 * n)], uy)
    z2, y4, left0, *uy = both(send(half(z1), ALONG_Y), send(half(y3), ALONG_Z), left0, *uy)
    p2, o4 = send(z2, PAIR), send(y4, PAIR)
    uz = select(after(hot_z, z2), [zf, z1, p1], [(0, k), (k, 2 * k), (3 * k, 4 * k)])
    spans = ((2 * k, 3 * k), (4 * n, 5 * n))
    z_parts, y_parts = (*uz, z2, p2), (*uy, y4, o4)
    return update(
        ids, (hot_z, hot_y), spans, z_parts, y_parts, (left0, left1), lower, fin, matrix
    )


def solution(mesh):
    return jax.shard_map(
        on_device,
        mesh=mesh,
        in_specs=(P("prow", "pcol"), P()),
        out_specs=P("prow", "pcol"),
        check_vma=False,
    )
```

```python
import functools
import jax
import jax.numpy as jnp
from jax import lax
from jax.experimental import pallas as pl
from jax.experimental.pallas import tpu as pltpu
from jax.sharding import PartitionSpec as P

NB = 256
NEWTON = 3
ZN, YN = 8, 4
CAP = 8
SLOTS = 2 * CAP
CHIP = 2 * SLOTS
WZ = 2048
F32 = jnp.float32
BF16 = jnp.bfloat16
VMEM = pl.BlockSpec(memory_space=pltpu.VMEM)
SMEM = pl.BlockSpec(memory_space=pltpu.SMEM)
ANY = pl.BlockSpec(memory_space=pl.ANY)
HBM = pl.BlockSpec(memory_space=pltpu.HBM)
PARAMS = pltpu.CompilerParams(vmem_limit_bytes=16 * 2**20)


def moves(dz, dy):
    pairs = []
    for z in range(ZN):
        for y in range(YN):
            for core in range(2):
                sign = 1 - 2 * core
                there = ((z + sign * dz) % ZN) * YN + (y + sign * dy) % YN
                pairs.append(((z * YN + y) * 2 + core, there * 2 + core))
    return pairs


ALONG_Z = moves(1, 0)
ALONG_Y = moves(0, 1)
TWICE_Y = moves(0, 2)
PAIR = [(i, i ^ 1) for i in range(2 * ZN * YN)]


NEAR = [(0, 1), (1, 0), (2, 3), (3, 2)]
FAR = [(0, 3), (1, 2), (2, 1), (3, 0)]
SKIP = [(0, 2), (1, 3), (2, 0), (3, 1)]


def over(array, pairs):
    return lax.ppermute(array, "pcol", pairs)


def send(array, pairs):
    return lax.ppermute(array, "prow", pairs)


def after(array, *others):
    return lax.optimization_barrier((array, *others))[0]


def both(*arrays):
    return lax.optimization_barrier(arrays)


def iota(shape, dim):
    return lax.broadcasted_iota(jnp.int32, shape, dim)


def to_column(row):
    n = row.shape[1]
    eye = iota((n, n), 0) == iota((n, n), 1)
    return jnp.sum(jnp.where(eye, row, 0.0), axis=1, keepdims=True)


def slot_column(piv_row, rows_dev):
    n = piv_row.shape[1]
    owner_row = lax.div(piv_row, jnp.int32(rows_dev)).astype(F32)
    owner_col = to_column(owner_row)
    before = iota((n, n), 1) < iota((n, n), 0)
    rank = jnp.sum(jnp.where(before & (owner_row == owner_col), 1.0, 0.0), axis=1, keepdims=True)
    return owner_col * CAP + rank


def chip_slots(me, order):
    n = ZN * YN * SLOTS
    pos = iota((1, n), 1)
    block = pos // SLOTS
    chip = me // 2
    z, y = chip // YN, chip % YN
    sign = 2 * (me % 2) - 1
    if order == "z first":
        zz = (z - block % ZN) & (ZN - 1)
        yy = (y + sign * (block // ZN)) & (YN - 1)
    else:
        yy = (y - block % YN) & (YN - 1)
        zz = (z + sign * (block // YN)) & (ZN - 1)
    return ((zz * YN + yy) * SLOTS + pos % SLOTS).astype(F32)


def is_pivot(piv_row, me, rows_dev):
    local = piv_row - me * rows_dev
    hit = iota((rows_dev, piv_row.shape[1]), 0) == local
    return jnp.max(jnp.where(hit, 1.0, 0.0), axis=1, keepdims=True) > 0.5


def list_rows(blocks, which):
    parts = []
    for block in blocks:
        rows, width = block.shape
        chips = rows // CHIP
        parts.append(block.reshape(chips, 2, SLOTS, width)[:, which].reshape(chips * SLOTS, width))
    return jnp.concatenate(parts, axis=0) if len(parts) > 1 else parts[0]


def dot(a, b):
    return jnp.dot(a, b, preferred_element_type=F32)


def pieces(b):
    high = b.astype(BF16)
    rest = b - high.astype(F32)
    middle = rest.astype(BF16)
    return high, middle, (rest - middle.astype(F32)).astype(BF16)


def dot_exact(a, parts):
    high, middle, low = parts
    return dot(a, high) + (dot(a, middle) + dot(a, low))


def pick_kernel(chunk, ids, piv_ref, a_hbm, out_ref, a_ref, sems):
    me = ids[0]
    chunks, rows_dev, _ = a_ref.shape

    def fetch(k):
        return pltpu.make_async_copy(
            a_hbm.at[:, pl.ds(k * chunk, chunk)], a_ref.at[k], sems.at[k]
        )

    for k in range(chunks):
        fetch(k).start()
    hots = []
    for which in range(2):
        piv_row = piv_ref[which : which + 1, :]
        n = piv_row.shape[1]
        owner_row = lax.div(piv_row, jnp.int32(rows_dev)).astype(F32)
        owner_col = to_column(owner_row)
        before = iota((n, n), 0) < iota((n, n), 1)
        rank = jnp.sum(jnp.where(before & (owner_row == owner_col), 1.0, 0.0), axis=0, keepdims=True)
        slot = rank + ((me % 2) * CAP).astype(F32)
        mine = owner_row == me.astype(F32)
        place = mine & (iota((SLOTS, n), 0).astype(F32) == slot)
        local = to_column((piv_row - me * rows_dev).astype(F32))
        row = local == iota((n, rows_dev), 1).astype(F32)
        hot = dot(jnp.where(place, 1.0, 0.0).astype(BF16), jnp.where(row, 1.0, 0.0).astype(BF16))
        hots.append(hot)
    hot = jnp.concatenate(hots, axis=0).astype(BF16)
    for k in range(chunks):
        fetch(k).wait()
        out_ref[:, k * chunk : (k + 1) * chunk] = dot(hot, a_ref[k]).astype(BF16)


def pick(ids, pivots, matrix):
    rows_dev, width = matrix.shape
    chunk = 1024
    chunks = width // chunk
    return pl.pallas_call(
        functools.partial(pick_kernel, chunk),
        in_specs=[SMEM, VMEM, HBM],
        out_specs=VMEM,
        out_shape=jax.ShapeDtypeStruct((CHIP, width), BF16),
        scratch_shapes=[
            pltpu.VMEM((chunks, rows_dev, chunk), BF16),
            pltpu.SemaphoreType.DMA((chunks,)),
        ],
        compiler_params=PARAMS,
        cost_estimate=pl.CostEstimate(
            flops=2 * CHIP * rows_dev * width, bytes_accessed=4 * rows_dev * width, transcendentals=0
        ),
        name="pick",
    )(ids, pivots, pltpu.with_memory_space_constraint(matrix, pltpu.HBM))


def maps_kernel(rows_dev, ids, piv_ref, *out_refs):
    me = ids[0]
    for which in range(2):
        slots = slot_column(piv_ref[which : which + 1, :], rows_dev)
        rows = slice(which * NB, (which + 1) * NB)
        for order, out in zip(("z first", "y first"), out_refs):
            out[rows, :] = jnp.where(slots == chip_slots(me, order), 1.0, 0.0).astype(BF16)


def maps(ids, pivots, rows_dev):
    shape = jax.ShapeDtypeStruct((2 * NB, ZN * YN * SLOTS), BF16)
    return pl.pallas_call(
        functools.partial(maps_kernel, rows_dev),
        in_specs=[SMEM, VMEM],
        out_specs=[VMEM] * 2,
        out_shape=[shape] * 2,
        cost_estimate=pl.CostEstimate(flops=2**30, bytes_accessed=2**22, transcendentals=0),
        name="maps",
    )(ids, pivots)


def inverse(block):
    n = block.shape[0]
    wide = block.astype(F32)
    eye = iota((n, n), 0) == iota((n, n), 1)
    diagonal_row = jnp.sum(jnp.where(eye, wide, 0.0), axis=0, keepdims=True)
    diagonal_col = jnp.sum(jnp.where(eye, wide, 0.0), axis=1, keepdims=True)
    twice = jnp.where(eye, 2.0, 0.0)
    guess = (1.0 / diagonal_col) * (twice - wide * (1.0 / diagonal_row))
    for step in range(NEWTON - 1):
        parts = pieces(guess)
        rest_high, rest_low, _ = pieces(0.5 * twice - dot_exact(block, parts))
        change = dot(parts[0], rest_low) + dot(parts[1], rest_high)
        guess = guess + (dot(parts[0], rest_high) + change)
    return guess


def factor_kernel(ids, piv_ref, s0_ref, s1_ref, pan0_ref, pan1_ref, l0_ref, l1_ref, lp_ref, fin_ref):
    me, col = ids[0], ids[1]
    rows_dev = pan0_ref.shape[0]
    upper01 = s1_ref[:NB, :]
    inv0 = pieces(inverse(s0_ref[:NB, :]))
    lower = dot_exact(s0_ref[NB:, :], inv0).astype(BF16)
    lp_ref[...] = lower
    block1 = (s1_ref[NB:, :].astype(F32) - dot(lower, upper01)).astype(BF16)
    inv1 = pieces(inverse(block1))
    live0 = jnp.logical_not(is_pivot(piv_ref[0:1, :], me, rows_dev))
    live1 = live0 & jnp.logical_not(is_pivot(piv_ref[1:2, :], me, rows_dev))
    pan0 = pan0_ref[...]
    left0 = jnp.where(live0, dot_exact(pan0, inv0), 0.0).astype(BF16)
    l0_ref[...] = left0
    pan1 = (pan1_ref[...].astype(F32) - dot(left0, upper01)).astype(BF16)
    left1 = jnp.where(live1, dot_exact(pan1, inv1), 0.0).astype(BF16)
    l1_ref[...] = left1
    fin0 = jnp.where(live0, left0.astype(F32), pan0.astype(F32))
    fin1 = jnp.where(live1, left1.astype(F32), pan1.astype(F32))
    fin_ref[...] = jnp.where(col == 0, fin0, fin1).astype(BF16)


def factor(ids, pivots, uppers, pan0, pan1):
    rows_dev = pan0.shape[0]
    left = jax.ShapeDtypeStruct((rows_dev, NB), BF16)
    return pl.pallas_call(
        factor_kernel,
        in_specs=[SMEM] + [VMEM] * 5,
        out_specs=[VMEM] * 4,
        out_shape=[left, left, jax.ShapeDtypeStruct((NB, NB), BF16), left],
        compiler_params=PARAMS,
        cost_estimate=pl.CostEstimate(
            flops=2 * 3 * 64 * NB**3, bytes_accessed=4 * 2**20, transcendentals=0
        ),
        name="factor",
    )(ids, pivots, *uppers, pan0, pan1)


def assemble_kernel(ids, near_ref, own_ref, other_ref, far_ref, all_ref):
    even = ids[0] % 2 == 0
    n = CHIP
    own, other = own_ref[...], other_ref[...]
    down, up = jnp.where(even, own, other), jnp.where(even, other, own)
    order = [near_ref[...], down, far_ref[...], up[2 * n :], up[n : 2 * n], up[:n]]
    all_ref[...] = jnp.concatenate(order, axis=0)


def assemble(ids, near, own, other, far):
    width = near.shape[1]
    return pl.pallas_call(
        assemble_kernel,
        in_specs=[SMEM] + [VMEM] * 4,
        out_specs=VMEM,
        out_shape=jax.ShapeDtypeStruct((ZN * CHIP, width), BF16),
        compiler_params=PARAMS,
        cost_estimate=pl.CostEstimate(flops=2**20, bytes_accessed=2**20, transcendentals=0),
        name="assemble",
    )(ids, near, own, other, far)


def step_of(width):
    if width < 512:
        return width
    return 640 if width % 1280 == 0 else 512


def select_kernel(gap, gap_rows, hot_ref, *refs):
    blocks, outs = refs[:-2], refs[-2:]
    width = outs[0].shape[1]
    step = step_of(width)
    for at in range(0, width, step):
        cols = slice(at, at + step)
        parts = [block[:, cols] for block in blocks]
        for which, out in enumerate(outs):
            rows = list_rows(parts[:gap], which)
            if gap_rows:
                none = jnp.zeros((gap_rows, step), BF16)
                rows = jnp.concatenate([rows, none, list_rows(parts[gap:], which)], axis=0)
            hot = hot_ref[which * NB : (which + 1) * NB, :]
            out[:, cols] = dot(hot, rows).astype(BF16)


def select(hot, blocks, gap=None, gap_rows=0):
    width = blocks[0].shape[1]
    shape = jax.ShapeDtypeStruct((NB, width), BF16)
    slots = ZN * YN * SLOTS - gap_rows
    return pl.pallas_call(
        functools.partial(select_kernel, gap, gap_rows),
        in_specs=[VMEM] * (1 + len(blocks)),
        out_specs=[VMEM, VMEM],
        out_shape=[shape, shape],
        compiler_params=PARAMS,
        cost_estimate=pl.CostEstimate(
            flops=2 * 2 * NB * slots * width, bytes_accessed=2**20, transcendentals=0
        ),
        name="select",
    )(hot, *blocks)


def update_kernel(
    spans, ids, hotz_ref, hoty_ref, uz0, uz1, z_mine, z_other, uy0, uy1, y_mine, y_other,
    l0_ref, l1_ref, lp_ref, fin_ref, a_ref, out_hbm, out_ref, sems,
):
    me, col = ids[0], ids[1]
    puts = []
    start = 0
    for span, hot_ref, u0_ref, u1_ref, mine_ref, other_ref in (
        (spans[0], hotz_ref, uz0, uz1, z_mine, z_other),
        (spans[1], hoty_ref, uy0, uy1, y_mine, y_other),
    ):
        width = u0_ref.shape[1]
        half = width // 2
        step = step_of(width)
        for at in range(0, width, step):
            side = at // half
            cols = slice(at, at + step)
            near = slice(at - side * half, at - side * half + step)
            whole = slice(start + at, start + at + step)
            last = jnp.where(me % 2 == side, mine_ref[:, near], other_ref[:, near])
            u0 = u0_ref[:, cols].astype(F32) + dot(hot_ref[:NB, span], list_rows([last], 0))
            u0 = u0.astype(BF16)
            u1 = u1_ref[:, cols].astype(F32) + dot(hot_ref[NB:, span], list_rows([last], 1))
            u1 = (u1 - dot(lp_ref[...], u0)).astype(BF16)
            a = (a_ref[:, whole].astype(F32) - dot(l0_ref[...], u0)).astype(BF16)
            out_ref[:, whole] = (a.astype(F32) - dot(l1_ref[...], u1)).astype(BF16)
            if start + at == 0:

                @pl.when(col < 2)
                def _():
                    out_ref[:, :NB] = fin_ref[...]

            put = pltpu.make_async_copy(
                out_ref.at[:, whole], out_hbm.at[:, whole], sems.at[len(puts)]
            )
            put.start()
            puts.append(put)
        start += width
    for put in puts:
        put.wait()


def update(ids, hots, spans, z_parts, y_parts, lefts, lower, fin, matrix):
    rows_dev, columns = matrix.shape
    steps = sum(parts[0].shape[1] // step_of(parts[0].shape[1]) for parts in (z_parts, y_parts))
    return pl.pallas_call(
        functools.partial(update_kernel, [slice(*span) for span in spans]),
        in_specs=[SMEM] + [VMEM] * 15,
        out_specs=ANY,
        out_shape=jax.ShapeDtypeStruct((rows_dev, columns), BF16),
        scratch_shapes=[pltpu.VMEM((rows_dev, columns), BF16), pltpu.SemaphoreType.DMA((steps,))],
        compiler_params=PARAMS,
        cost_estimate=pl.CostEstimate(
            flops=2 * columns * NB * (2 * 128 + NB + 2 * rows_dev),
            bytes_accessed=4 * columns * rows_dev,
            transcendentals=0,
        ),
        name="update",
    )(ids, *hots, *z_parts, *y_parts, *lefts, lower, fin, matrix)


def on_device(matrix, pivots):
    rows_dev, width = matrix.shape
    me = lax.axis_index("prow")
    col = lax.axis_index("pcol")
    ids = jnp.stack([me, col]).astype(jnp.int32)
    even = me % 2 == 0

    def panels(array, near, far, across):
        zero = jnp.where(col == 0, array, jnp.where(col == 1, near, jnp.where(col == 3, far, across)))
        one = jnp.where(col == 1, array, jnp.where(col == 0, near, jnp.where(col == 2, far, across)))
        return zero, one

    def half(array):
        width = array.shape[1] // 2
        return jnp.where(even, array[:, :width], array[:, width:])

    packed = pick(ids, pivots, matrix)
    packed = packed + send(packed, PAIR)
    zb, yb = packed[:, :WZ], packed[:, WZ:]
    n = CHIP

    hot_z, hot_y = maps(ids, pivots, rows_dev)
    t1, r1, hot_z, hot_y = both(send(zb, ALONG_Z), send(yb, ALONG_Y), hot_z, hot_y)

    panel = after(matrix[:, :NB], t1)
    near, far = over(panel, NEAR), over(panel, FAR)
    t2, r2, q1 = both(send(t1, ALONG_Z), send(r1, ALONG_Y), send(r1, PAIR))
    yf = jnp.concatenate([yb, jnp.where(even, r1, q1), r2, jnp.where(even, q1, r1)], axis=0)

    y1 = send(yf, ALONG_Z)
    t3, near, far = both(send(t2, ALONG_Z), near, far)
    own = jnp.concatenate([t1, t2, t3], axis=0)
    t4, oth, y1 = both(send(t3, ALONG_Z), send(own, PAIR), y1)

    own_first, oth_first = own[:, :NB], oth[:, :NB]
    down, up = jnp.where(even, own_first, oth_first), jnp.where(even, oth_first, own_first)
    order = [zb[:, :NB], down, t4[:, :NB], up[2 * n :], up[n : 2 * n], up[:n]]
    v0 = jnp.concatenate(order, axis=0)
    zf = assemble(after(ids, v0), zb, own, oth, t4)
    across = over(far, NEAR)
    v1, v2, across = both(send(v0, ALONG_Y), send(half(v0), TWICE_Y), across)
    z1 = send(after(zf, v1), ALONG_Y)
    w = send(jnp.concatenate([v1, v2], axis=1), PAIR)
    w1, w2 = w[:, :NB], w[:, NB:]
    opposite = jnp.concatenate([jnp.where(even, v2, w2), jnp.where(even, w2, v2)], axis=1)
    k = ZN * SLOTS
    entries = select(hot_z, [v0, v1, opposite, w1])
    y2, o1, *entries = both(send(y1, ALONG_Z), send(y1, PAIR), *entries)
    pan0, pan1 = panels(panel, near, far, across)

    part = jnp.where(even, entries[0], entries[1])
    part = panels(part, over(part, NEAR), over(part, FAR), over(part, SKIP))
    part = jnp.concatenate(part, axis=1)
    y3, z1, o2, part = both(send(y2, ALONG_Z), z1, send(y2, PAIR), part)

    rest = send(part, PAIR)
    uppers = jnp.concatenate([jnp.where(even, part, rest), jnp.where(even, rest, part)], axis=0)
    uppers = [uppers[:, :NB], uppers[:, NB:]]
    left0, left1, lower, fin = factor(ids, pivots, uppers, pan0, pan1)
    p1, o3 = send(z1, PAIR), send(y3, PAIR)
    n = YN * SLOTS
    uy = select(hot_y, [yf, y1, y2, y3, o3, o2, o1], 4, n)
    z2, y4, left0, *uy = both(send(half(z1), ALONG_Y), send(half(y3), ALONG_Z), left0, *uy)
    p2, o4 = send(z2, PAIR), send(y4, PAIR)
    uz = select(after(hot_z, z2), [zf, z1, p1], 2, k)
    spans = ((2 * k, 3 * k), (4 * n, 5 * n))
    z_parts, y_parts = (*uz, z2, p2), (*uy, y4, o4)
    return update(
        ids, (hot_z, hot_y), spans, z_parts, y_parts, (left0, left1), lower, fin, matrix
    )


def solution(mesh):
    return jax.shard_map(
        on_device,
        mesh=mesh,
        in_specs=(P("prow", "pcol"), P()),
        out_specs=P("prow", "pcol"),
        check_vma=False,
    )
```
